256 devices in a mesh: group: 4 (over y), dev: 64 (over z, x, core).
Axes of the slice: x: 4, y: 4, z: 8, core: 2. Of those that a mesh axis runs over, the one named last changes fastest.
Arguments:
- tokens: bfloat16 [32768, 5120], P(('group', 'dev')), may hold values from -6 to 6
- cotangent: bfloat16 [32768, 5120], P(('group', 'dev')), may hold values from -6 to 6
- routes: int32 [32768, 1], P(('group', 'dev')), may hold values from 0 to 7; in each aligned block of 128 rows (0 to 127, 128 to 255, ...) at most 20 rows name the same one
- codes: bfloat16 [3, 6144, 5120], P(None, 'dev', 'group'), may hold values from -0.078125 to 0.078125
- scales: float32 [3, 6144, 40], P(None, 'dev', 'group'), may hold values from 0.5 to 2
- first_moment: float32 [3, 6144, 5120], P(None, 'dev', 'group'), may hold values from -18 to 18
- second_moment: float32 [3, 6144, 5120], P(None, 'dev', 'group'), may hold values from 0.2 to 5
Outputs:
- grad_tokens: bfloat16 [32768, 5120], P(('group', 'dev'))
- new_weights: float32 [3, 6144, 5120], P(None, 'dev', 'group')
- new_first: float32 [3, 6144, 5120], P(None, 'dev', 'group')
- new_second: float32 [3, 6144, 5120], P(None, 'dev', 'group')
The draws below stay inside these ranges and needn't reach their ends.
Inputs may be any that keep to these rules, and one draw needn't show every extreme that they name: `routes`: among the rows of one device, no expert is named by more than 20 rows; in every draw some expert is named by exactly 20 rows of some device.
All inputs are finite; a program needn't handle non-finite values.
Results may differ from the reference program's by a relative error of at most 0.018.
Values may be sent and summed in bfloat16 or wider, within the bound.
A program may use at most 128 MiB of HBM per device.

```python
import math
import jax
import jax.numpy as jnp
import numpy as np
from jax import lax

D = 5120
H_WIN = 768
SLICES = 4
COPIES = 2
QB = 128
ROWS_DEV = 128
EXPERTS = 8
HID_DEV = 192
CAP = 20
HALF = 10
TOKENS = 32768
N_GROUP = 4
N_DEV = 64


def levels(own_key, extent, split, low, largest):
    level = 1.0
    for axis_at, blocks in split:
        heights = jax.random.uniform(jax.random.fold_in(jax.random.fold_in(own_key, 6), axis_at), (blocks,), jnp.float32, low / len(split), largest / len(split))
        level = level * jnp.repeat(jnp.exp(heights), extent[axis_at] // blocks).reshape((-1,) + (1,) * (len(extent) - 1 - axis_at))
    return level


def routed_block(key, own, number, rows, count, top, bound, lean):
    ranking = jax.random.permutation(key, count)
    packed, usual = portions_of(count, rows * top, bound, lean, True), portions_of(count, rows * top, bound, lean, False)
    places = jnp.arange(count)

    def named(tallies, offset_by):
        used = int((tallies > 0).sum())
        fixed = max(1, used // 4)
        passed = fixed + (places - fixed + offset_by * (used - fixed)) % max(1, count - fixed)
        return jnp.zeros((count,), jnp.int32).at[ranking[jnp.where(places < fixed, places, passed)]].set(jnp.asarray(tallies, jnp.int32))

    tallies = jnp.where(number % 4 == 0, named(packed, number // 4), named(usual, number - number // 4 - 1))
    mixed = jax.random.permutation(jax.random.fold_in(own, 3), count)
    giver, sink = mixed[0:count // 2 * 2:2], mixed[1:count // 2 * 2:2]
    room = jnp.minimum(tallies[giver] - 1, bound - tallies[sink]) // 2
    room = jnp.where((giver == ranking[0]) | (sink == ranking[0]) | (tallies[sink] == 0), 0, jnp.maximum(room, 0))
    passed = jax.random.randint(jax.random.fold_in(own, 4), (count // 2,), 0, 1 << 20) % (room + 1)
    tallies = tallies.at[giver].add(-passed).at[sink].add(passed)
    labels = jnp.searchsorted(jnp.cumsum(tallies), jnp.arange(rows * top), side="right").astype(jnp.int32)
    listing = labels.reshape(top, rows).T
    listing = listing[jax.random.permutation(jax.random.fold_in(own, 1), rows)]
    offset_by = jax.random.randint(jax.random.fold_in(own, 2), (rows, 1), 0, top)
    return jnp.take_along_axis(listing, (jnp.arange(top)[None, :] + offset_by) % top, axis=1)


def portions_of(amount, total, limit, skew, full):
    weights = [(1 << 20) // math.isqrt(standing ** skew) + 1 for standing in range(1, amount + 1)]
    largest = limit if full else min(limit, max(-(-total // amount), total * weights[0] // sum(weights)))
    least = 1 if total - largest >= amount - 1 else 0
    holding, rest = [largest] + [least] * (amount - 1), total - largest - least * (amount - 1)
    while rest > 0:
        free = [i for i in range(1, amount) if holding[i] < largest] or [i for i in range(1, amount) if holding[i] < limit]
        pool, remaining = sum([weights[i] for i in free]), rest
        for i in free:
            extra = min(limit - holding[i], max(1, remaining * weights[i] // pool), rest)
            holding[i] = holding[i] + extra
            rest = rest - extra
    return np.array(holding)


def gaussian(key, shape, width, reach, cuts=(), kind=jnp.bfloat16):
    result = jax.random.normal(key, shape, jnp.float32) * width
    if len(cuts) > 0:
        result = levels(key, shape, cuts, -0.22, 0.18) * result
    return jnp.clip(result, min=-reach, max=reach).astype(kind)


def setup_inputs(seed: int = 0) -> dict:
    keys = jax.random.split(jax.random.key(seed), 8)
    tokens = gaussian(keys[0], (TOKENS, D), 1.0, 6.0, ((0, 256),))
    cotangent = gaussian(keys[1], (TOKENS, D), 1.0, 6.0, ((0, 256),))
    routes_keys = jax.random.split(jax.random.fold_in(keys[2], 1), TOKENS // ROWS_DEV)
    routes_turns = jax.random.permutation(jax.random.fold_in(keys[2], 3), TOKENS // ROWS_DEV)
    routes = jax.vmap(lambda own, number: routed_block(jax.random.fold_in(keys[2], 2), own, number, ROWS_DEV, EXPERTS, 1, CAP, 2))(routes_keys, routes_turns).reshape((TOKENS, 1))
    codes = gaussian(keys[3], (3, EXPERTS * H_WIN, D), D ** -0.5, 0.078125, ((1, 64), (2, 4)))
    scales = jnp.clip(jnp.exp(math.log(2.0) - 1.3862944 * jax.random.uniform(keys[4], (3, EXPERTS * H_WIN, D // QB), jnp.float32) ** levels(keys[4], (3, EXPERTS * H_WIN, D // QB), ((1, 64), (2, 4)), -0.2, 0.2)), 0.5, 2.0)
    first_moment = gaussian(keys[5], (3, EXPERTS * H_WIN, D), 3.0, 18.0, ((1, 64), (2, 4)), jnp.float32)
    second_moment = jnp.clip(jnp.exp(math.log(5.0) - 3.218876 * jax.random.uniform(keys[6], (3, EXPERTS * H_WIN, D), jnp.float32) ** levels(keys[6], (3, EXPERTS * H_WIN, D), ((1, 64), (2, 4)), -0.2, 0.2)), 0.2, 5.0)
    return {"tokens": tokens, "cotangent": cotangent, "routes": routes, "codes": codes, "scales": scales, "first_moment": first_moment, "second_moment": second_moment}


BETA_ONE = 0.9
BETA_TWO = 0.999
LEARNING_RATE = 0.01
ADAM_EPS = 1e-08
STEP_COUNT = 10

def slot_positions(route_rows):
    matches = route_rows[:, :, None] == jnp.arange(EXPERTS, dtype=jnp.int32)[None, None, :]
    counted = matches.astype(jnp.int32)
    earlier = jnp.cumsum(counted, axis=1) - counted
    return lax.optimization_barrier(jnp.sum(jnp.where(matches, earlier, 0), axis=2)).astype(jnp.int32)

def contract_rows(first_op, second_op):
    return lax.dot_general(first_op, second_op, (((0,), (0,)), ((), ())), preferred_element_type=jnp.float32)

def contract_cols(first_op, second_op):
    return lax.dot_general(first_op, second_op, (((1,), (1,)), ((), ())), preferred_element_type=jnp.float32)

def round_trip(values):
    return lax.optimization_barrier(values.astype(jnp.bfloat16)).astype(jnp.float32)

def expert_half(inbound, cot_inbound, gate_weight, upward_weight, down_weight):
    gate_proj = contract_cols(inbound, gate_weight)
    upward = contract_cols(inbound, upward_weight)
    sigmoid_gate = jax.nn.sigmoid(gate_proj)
    activated = gate_proj * sigmoid_gate
    hidden = (activated * upward).astype(jnp.bfloat16)
    hidden_cot = contract_cols(cot_inbound, down_weight)
    gate_cot = (hidden_cot * upward * sigmoid_gate * (1.0 + gate_proj * (1.0 - sigmoid_gate))).astype(jnp.bfloat16)
    upward_cot = (hidden_cot * activated).astype(jnp.bfloat16)
    down_grad = round_trip(contract_rows(hidden, cot_inbound))
    gate_grad = round_trip(contract_rows(gate_cot, inbound))
    upward_grad = round_trip(contract_rows(upward_cot, inbound))
    summed = jnp.zeros((inbound.shape[0], D), jnp.float32)
    for piece_number in range(SLICES):
        low_unit = piece_number * HID_DEV
        slice_term = jnp.dot(gate_cot[:, low_unit:low_unit + HID_DEV], gate_weight[low_unit:low_unit + HID_DEV], preferred_element_type=jnp.float32)
        slice_term = slice_term + jnp.dot(upward_cot[:, low_unit:low_unit + HID_DEV], upward_weight[low_unit:low_unit + HID_DEV], preferred_element_type=jnp.float32)
        summed = summed + round_trip(slice_term)
    return (summed, jnp.stack([gate_grad, upward_grad, down_grad]))

def reference(tokens, cotangent, routes, codes, scales, first_moment, second_moment):
    full_weights = codes.astype(jnp.float32) * jnp.repeat(scales, QB, axis=2)
    weights = full_weights.astype(jnp.bfloat16)
    group_rows = N_DEV * ROWS_DEV
    slot_count = N_DEV * CAP
    source = jnp.arange(group_rows, dtype=jnp.int32) // ROWS_DEV
    gradient = jnp.zeros(full_weights.shape, jnp.float32)
    outputs = []
    for group_number in range(N_GROUP):
        row_start = group_number * group_rows
        inputs = tokens[row_start:row_start + group_rows]
        cot_rows = cotangent[row_start:row_start + group_rows]
        route_rows = routes[row_start:row_start + group_rows, 0]
        slot_ids = (source * CAP + slot_positions(route_rows.reshape(N_DEV, ROWS_DEV)).reshape(-1)).astype(jnp.int32)
        grad_input = jnp.zeros((group_rows, D), jnp.float32)
        for expert in range(EXPERTS):
            chosen = route_rows == expert
            target = jnp.where(chosen, slot_ids, slot_count).astype(jnp.int32)
            inbound = jnp.zeros((slot_count, D), jnp.bfloat16).at[target].set(inputs, mode='drop')
            cot_inbound = jnp.zeros((slot_count, D), jnp.bfloat16).at[target].set(cot_rows, mode='drop')
            unit_start = expert * H_WIN
            gate_weight = weights[0, unit_start:unit_start + H_WIN]
            upward_weight = weights[1, unit_start:unit_start + H_WIN]
            down_weight = weights[2, unit_start:unit_start + H_WIN]
            halves_in = inbound.reshape(N_DEV, COPIES, HALF, D)
            halves_cot = cot_inbound.reshape(N_DEV, COPIES, HALF, D)
            pieces = []
            for copy_number in range(COPIES):
                summed_half, expert_grads = expert_half(halves_in[:, copy_number].reshape(N_DEV * HALF, D), halves_cot[:, copy_number].reshape(N_DEV * HALF, D), gate_weight, upward_weight, down_weight)
                gradient = gradient.at[:, unit_start:unit_start + H_WIN].add(expert_grads)
                pieces.append(summed_half.reshape(N_DEV, HALF, D))
            summed = jnp.stack(pieces, axis=1).reshape(slot_count, D)
            picked = summed[jnp.minimum(slot_ids, slot_count - 1)]
            grad_input = grad_input + jnp.where(chosen[:, None], picked, jnp.float32(0.0))
        outputs.append(grad_input.astype(jnp.bfloat16))
    grad_tokens = jnp.concatenate(outputs, axis=0)
    new_first = BETA_ONE * first_moment + (1.0 - BETA_ONE) * gradient
    new_second = BETA_TWO * second_moment + (1.0 - BETA_TWO) * gradient * gradient
    first_fix = 1.0 - BETA_ONE ** STEP_COUNT
    second_fix = 1.0 - BETA_TWO ** STEP_COUNT
    new_weights = full_weights - LEARNING_RATE * (new_first / first_fix) / (jnp.sqrt(new_second / second_fix) + ADAM_EPS)
    return (grad_tokens, new_weights, new_first, new_second)
```

```python
import jax
import jax.numpy as jnp
from jax import lax
from jax.experimental import pallas as pl
from jax.experimental.pallas import tpu as pltpu
from jax.sharding import PartitionSpec as P

MESH = pl.DeviceIdType.MESH
QB = 128
NZ, NX, NY = 8, 4, 4
CAP = 20
SLAB = 2 * CAP
NEAR = (1, 7, 2, 6, 3, 5, 4)
HBM = pl.BlockSpec(memory_space=pltpu.HBM)

BETA_ONE = 0.9
BETA_TWO = 0.999
LEARNING_RATE = 0.01
ADAM_EPS = 1e-08
STEP_COUNT = 10


def place():
    dev = lax.axis_index("dev")
    return lax.axis_index("group"), dev // 8, (dev // 2) % 4, dev % 2


def device(y, z, x, c):
    return (y, (z * NX + x) * 2 + c)


def along_z(k):
    y, z, x, c = place()
    return device(y, (z + k) % NZ, x, c)


def along_y(k):
    y, z, x, c = place()
    return device((y + k) % NY, z, x, c)


def token_pair():
    y, z, x, c = place()
    return device(y, z, x + 1 - 2 * (x % 2), c)


def weight_pair():
    y, z, x, c = place()
    return device(y, z, 3 - x, c)


def other_core():
    y, z, x, c = place()
    return device(y, z, x, 1 - c)


def greet(peers):
    barrier = pltpu.get_barrier_semaphore()
    for peer in peers:
        pl.semaphore_signal(barrier, inc=1, device_id=peer, device_id_type=MESH)
    pl.semaphore_wait(barrier, len(peers))


def dispatch_kernel(slabs, owned, rows, weights, z_send, z_recv, x_send, x_recv, c_send, c_recv, w_send, w_recv, local):
    y = lax.axis_index("group")
    width = owned.shape[2]
    greet(
        [along_z(k) for k in range(1, NZ)]
        + [along_y(k) for k in range(1, NY)]
        + [token_pair(), weight_pair(), other_core()]
    )

    def remote(src, dst, send, recv, peer):
        copy = pltpu.make_async_remote_copy(
            src, dst, send, recv, device_id=peer, device_id_type=MESH
        )
        copy.start()
        return copy

    mine = pl.ds(pl.multiple_of(y * width, width), width)
    to_z = {}
    for k in NEAR:
        to_z[k] = remote(slabs.at[k], rows.at[0, 0, k], z_send.at[k], z_recv.at[k], along_z(k))
    keep_rows = pltpu.make_async_copy(slabs.at[0], rows.at[0, 0, 0], local.at[0])
    keep_rows.start()
    keep_weights = pltpu.make_async_copy(owned, weights.at[:, 0, :, mine], local.at[1])
    keep_weights.start()
    to_partner = remote(owned, weights.at[:, 1, :, mine], w_send.at[0], w_recv.at[0], weight_pair())
    to_y = [
        remote(owned, weights.at[:, 0, :, mine], w_send.at[k], w_recv.at[k], along_y(k))
        for k in range(1, NY)
    ]

    to_x, to_c = [], []

    def spread(k):
        to_x.append(
            remote(rows.at[0, 0, k], rows.at[0, 1, k], x_send.at[k], x_recv.at[k], token_pair())
        )
        to_c.append(
            remote(rows.at[0, 0, k], rows.at[1, 0, k], c_send.at[0, k], c_recv.at[0, k], other_core())
        )

    def cross(at, k):
        to_x[at].wait_recv()
        to_c.append(
            remote(rows.at[0, 1, k], rows.at[1, 1, k], c_send.at[1, k], c_recv.at[1, k], other_core())
        )

    keep_rows.wait()
    spread(0)
    to_partner.wait_recv()
    for k in range(1, NY):
        to_y.append(
            remote(
                weights.at[:, 1, :, mine],
                weights.at[:, 1, :, mine],
                w_send.at[NY - 1 + k],
                w_recv.at[NY - 1 + k],
                along_y(k),
            )
        )
    order = (0,) + NEAR
    for at in range(1, NZ):
        to_z[order[at]].wait_recv()
        spread(order[at])
        cross(at - 1, order[at - 1])
    cross(NZ - 1, order[NZ - 1])
    keep_weights.wait()
    to_partner.wait_send()
    for copy in to_y + to_c:
        copy.wait()
    for copy in to_x:
        copy.wait_send()
    for k in NEAR:
        to_z[k].wait_send()


def dispatch(slabs, owned):
    _, slab, features = slabs.shape
    dma = pltpu.SemaphoreType.DMA
    return pl.pallas_call(
        dispatch_kernel,
        out_shape=(
            jax.ShapeDtypeStruct((2, 2, NZ, slab, features), jnp.bfloat16),
            jax.ShapeDtypeStruct((3, 2, owned.shape[1], features), jnp.bfloat16),
        ),
        in_specs=[HBM, HBM],
        out_specs=(HBM, HBM),
        scratch_shapes=[
            dma((NZ,)),
            dma((NZ,)),
            dma((NZ,)),
            dma((NZ,)),
            dma((2, NZ)),
            dma((2, NZ)),
            dma((2 * NY - 1,)),
            dma((2 * NY - 1,)),
            dma((2,)),
        ],
        compiler_params=pltpu.CompilerParams(collective_id=0, has_side_effects=True),
        name="dispatch",
    )(slabs, owned)


def exchange(name, number, values, moves, results):
    peers = []
    for move in moves:
        if move[0] not in peers:
            peers.append(move[0])

    def kernel(*refs):
        sources = refs[: len(values)]
        targets = refs[len(values) : len(values) + len(results)]
        send, recv = refs[len(values) + len(results) :]
        greet([peer() for peer in peers])
        copies = []
        for at, (peer, source, source_index, target, target_index) in enumerate(moves):
            src, dst = sources[source], targets[target]
            if source_index is not None:
                src = src.at[source_index()]
            if target_index is not None:
                dst = dst.at[target_index()]
            copy = pltpu.make_async_remote_copy(
                src, dst, send.at[at], recv.at[at], device_id=peer(), device_id_type=MESH
            )
            copy.start()
            copies.append(copy)
        for copy in copies:
            copy.wait()

    return pl.pallas_call(
        kernel,
        out_shape=tuple(results),
        in_specs=[HBM] * len(values),
        out_specs=(HBM,) * len(results),
        scratch_shapes=[
            pltpu.SemaphoreType.DMA((len(moves),)),
            pltpu.SemaphoreType.DMA((len(moves),)),
        ],
        compiler_params=pltpu.CompilerParams(collective_id=number, has_side_effects=True),
        name=name,
    )(*values)


def peers_of(shift, count):
    return [(lambda k=k: shift(k)) for k in range(1, count)]


def shards(tokens, cotangent, routes, codes, scales, first_moment, second_moment):
    row_count, features = tokens.shape
    stored, width = codes.shape[1:]
    y, z, _, _ = place()
    owned_full = codes.astype(jnp.float32) * jnp.repeat(scales, QB, axis=2)
    owned = owned_full.astype(jnp.bfloat16)

    route_ids = routes[:, 0]
    matches = route_ids[:, None] == jnp.arange(NZ, dtype=jnp.int32)[None, :]
    counted = matches.astype(jnp.int32)
    earlier = jnp.cumsum(counted, axis=0) - counted
    position = jnp.sum(jnp.where(matches, earlier, 0), axis=1)
    ahead = (route_ids - z + NZ) % NZ
    row_range = jnp.arange(row_count, dtype=jnp.int32)
    slab_range = jnp.arange(NZ * SLAB, dtype=jnp.int32)
    packing = jnp.concatenate(
        [
            (slab_range[:, None] == (ahead * SLAB + position + half * CAP)[None, :])
            for half in (0, 1)
        ],
        axis=1,
    ).astype(jnp.bfloat16)
    both = jnp.concatenate([tokens, cotangent], axis=0)
    slabs = (
        jnp.dot(packing, both, preferred_element_type=jnp.float32)
        .astype(jnp.bfloat16)
        .reshape(NZ, SLAB, features)
    )

    rows, weights = dispatch(slabs, owned)
    units = 2 * stored
    pieces = 4 * NZ
    flat_rows = rows.reshape(pieces * SLAB, features)
    flat_weights = weights.reshape(3 * units, features)
    pre = lax.dot_general(
        flat_rows, flat_weights, (((1,), (1,)), ((), ())), preferred_element_type=jnp.float32
    ).reshape(pieces, SLAB, 3 * units)
    gate = pre[:, :CAP, :units]
    up = pre[:, :CAP, units : 2 * units]
    hidden_cot = pre[:, CAP:, 2 * units :]
    sig = jax.nn.sigmoid(gate)
    activated = gate * sig
    hidden = (activated * up).astype(jnp.bfloat16)
    gate_cot = (hidden_cot * up * sig * (1.0 + gate * (1.0 - sig))).astype(jnp.bfloat16)
    up_cot = (hidden_cot * activated).astype(jnp.bfloat16)
    cots = jnp.concatenate([gate_cot, up_cot], axis=2)
    blank = jnp.zeros_like(cots)
    mixed = jnp.concatenate(
        [
            jnp.concatenate([cots, jnp.zeros_like(hidden)], axis=2),
            jnp.concatenate([blank, hidden], axis=2),
        ],
        axis=1,
    ).reshape(pieces * SLAB, 3 * units)
    grads = (
        lax.dot_general(
            mixed, flat_rows, (((0,), (0,)), ((), ())), preferred_element_type=jnp.float32
        )
        .astype(jnp.bfloat16)
        .reshape(3, 2, stored, features)
    )
    half_width = features // 2
    spread = jnp.concatenate(
        [
            jnp.concatenate([cots, blank], axis=2),
            jnp.concatenate([blank, cots], axis=2),
        ],
        axis=1,
    ).reshape(pieces * SLAB, 4 * units)
    in_weights = flat_weights[: 2 * units]
    stacked = jnp.concatenate([in_weights[:, :half_width], in_weights[:, half_width:]], axis=0)
    terms = (
        jnp.dot(spread, stacked, preferred_element_type=jnp.float32)
        .astype(jnp.bfloat16)
        .reshape(2, 2, NZ, SLAB, half_width)
    )

    def total(first, *others):
        result = first.astype(jnp.float32)
        for other in others:
            result = result + other.astype(jnp.float32)
        return result

    slab_set = jax.ShapeDtypeStruct((2, NZ, SLAB, half_width), jnp.bfloat16)
    (crossed,) = exchange(
        "cores", 1, (terms,), [(other_core, 0, lambda: 1, 0, None)], [slab_set]
    )
    chip_terms = total(terms[0], crossed).astype(jnp.bfloat16)

    def columns(k):
        start = (lax.axis_index("group") + k) % NY * width
        return pl.ds(pl.multiple_of(start, width), width)

    def shares(matrices, number):
        return [
            (
                (lambda k=k: along_y(k)),
                number,
                (lambda k=k: (matrices, slice(None), slice(None), columns(k))),
                number,
                (lambda k=k: k - 1),
            )
            for k in range(1, NY)
        ]

    paired, first_shares = exchange(
        "pairs",
        2,
        (chip_terms, grads),
        [(token_pair, 0, lambda: 1, 0, None)] + shares(pl.ds(0, 2), 1),
        [
            jax.ShapeDtypeStruct((NZ, SLAB, half_width), jnp.bfloat16),
            jax.ShapeDtypeStruct((NY - 1, 2, 2, stored, width), jnp.bfloat16),
        ],
    )
    slot_grads = total(chip_terms[0], paired).astype(jnp.bfloat16)
    back = [
        ((lambda k=k: along_z(NZ - k)), 0, (lambda k=k: k), 0, (lambda k=k: k)) for k in NEAR
    ]
    returned, last_shares = exchange(
        "returns",
        3,
        (slot_grads, grads),
        back + shares(pl.ds(2, 1), 1),
        [
            jax.ShapeDtypeStruct((NZ, SLAB, half_width), jnp.bfloat16),
            jax.ShapeDtypeStruct((NY - 1, 1, 2, stored, width), jnp.bfloat16),
        ],
    )
    own_shares = lax.dynamic_slice_in_dim(grads, y * width, width, axis=3)
    summed = jnp.concatenate(
        [total(own_shares[:2], *first_shares), total(own_shares[2:], *last_shares)], axis=0
    )
    (given,) = exchange(
        "blocks",
        4,
        (summed[:, 1].astype(jnp.bfloat16),),
        [(weight_pair, 0, None, 0, None)],
        [jax.ShapeDtypeStruct((3, stored, width), jnp.bfloat16)],
    )
    gradient = summed[:, 0] + given.astype(jnp.float32)

    returned = jnp.concatenate([slot_grads[:1], returned[1:]], axis=0)
    flat_returned = returned.reshape(NZ * SLAB, half_width)
    grad_tokens = jnp.concatenate(
        [
            jnp.dot(
                ((ahead * SLAB + position + half * CAP)[:, None] == slab_range[None, :]).astype(
                    jnp.bfloat16
                ),
                flat_returned,
                preferred_element_type=jnp.float32,
            ).astype(jnp.bfloat16)
            for half in (0, 1)
        ],
        axis=1,
    )
    new_first = BETA_ONE * first_moment + (1.0 - BETA_ONE) * gradient
    new_second = BETA_TWO * second_moment + (1.0 - BETA_TWO) * gradient * gradient
    first_fix = 1.0 - BETA_ONE**STEP_COUNT
    second_fix = 1.0 - BETA_TWO**STEP_COUNT
    new_weights = owned_full - LEARNING_RATE * (new_first / first_fix) / (
        jnp.sqrt(new_second / second_fix) + ADAM_EPS
    )
    return (grad_tokens, new_weights, new_first, new_second)


def solution(mesh):
    stored = P(None, "dev", "group")
    spread = P(("group", "dev"), None)
    return jax.shard_map(
        shards,
        mesh=mesh,
        in_specs=(spread, spread, spread, stored, stored, stored, stored),
        out_specs=(spread, stored, stored, stored),
        check_vma=False,
    )
```

```python
import jax
import jax.numpy as jnp
from jax import lax
from jax.experimental import pallas as pl
from jax.experimental.pallas import tpu as pltpu
from jax.sharding import PartitionSpec as P

MESH = pl.DeviceIdType.MESH
QB = 128
NZ, NX, NY = 8, 4, 4
CAP = 20
SLAB = 2 * CAP
NEAR = (1, 7, 2, 6, 3, 5, 4)
HBM = pl.BlockSpec(memory_space=pltpu.HBM)

BETA_ONE = 0.9
BETA_TWO = 0.999
LEARNING_RATE = 0.01
ADAM_EPS = 1e-08
STEP_COUNT = 10


def place():
    dev = lax.axis_index("dev")
    return lax.axis_index("group"), dev // 8, (dev // 2) % 4, dev % 2


def device(y, z, x, c):
    return (y, (z * NX + x) * 2 + c)


def along_z(k):
    y, z, x, c = place()
    return device(y, (z + k) % NZ, x, c)


def along_y(k):
    y, z, x, c = place()
    return device((y + k) % NY, z, x, c)


def token_pair():
    y, z, x, c = place()
    return device(y, z, x + 1 - 2 * (x % 2), c)


def weight_pair():
    y, z, x, c = place()
    return device(y, z, 3 - x, c)


def other_core():
    y, z, x, c = place()
    return device(y, z, x, 1 - c)


def greet(peers):
    barrier = pltpu.get_barrier_semaphore()
    for peer in peers:
        pl.semaphore_signal(barrier, inc=1, device_id=peer, device_id_type=MESH)
    pl.semaphore_wait(barrier, len(peers))


def dispatch_kernel(slabs, owned, rows, weights, z_send, z_recv, x_send, x_recv, c_send, c_recv, w_send, w_recv, local):
    y = lax.axis_index("group")
    width = owned.shape[2]
    greet(
        [along_z(k) for k in range(1, NZ)]
        + [along_y(k) for k in range(1, NY)]
        + [token_pair(), weight_pair(), other_core()]
    )

    def remote(src, dst, send, recv, peer):
        copy = pltpu.make_async_remote_copy(
            src, dst, send, recv, device_id=peer, device_id_type=MESH
        )
        copy.start()
        return copy

    mine = pl.ds(pl.multiple_of(y * width, width), width)
    to_z = {}
    for k in NEAR:
        to_z[k] = remote(slabs.at[k], rows.at[0, 0, k], z_send.at[k], z_recv.at[k], along_z(k))
    keep_rows = pltpu.make_async_copy(slabs.at[0], rows.at[0, 0, 0], local.at[0])
    keep_rows.start()
    keep_weights = pltpu.make_async_copy(owned, weights.at[:, 0, :, mine], local.at[1])
    keep_weights.start()
    to_partner = remote(owned, weights.at[:, 1, :, mine], w_send.at[0], w_recv.at[0], weight_pair())
    to_y = [
        remote(owned, weights.at[:, 0, :, mine], w_send.at[k], w_recv.at[k], along_y(k))
        for k in range(1, NY)
    ]

    to_x, to_c = [], []

    def spread(k):
        to_x.append(
            remote(rows.at[0, 0, k], rows.at[0, 1, k], x_send.at[k], x_recv.at[k], token_pair())
        )
        to_c.append(
            remote(rows.at[0, 0, k], rows.at[1, 0, k], c_send.at[0, k], c_recv.at[0, k], other_core())
        )

    def cross(at, k):
        to_x[at].wait_recv()
        to_c.append(
            remote(rows.at[0, 1, k], rows.at[1, 1, k], c_send.at[1, k], c_recv.at[1, k], other_core())
        )

    keep_rows.wait()
    spread(0)
    to_partner.wait_recv()
    for k in range(1, NY):
        to_y.append(
            remote(
                weights.at[:, 1, :, mine],
                weights.at[:, 1, :, mine],
                w_send.at[NY - 1 + k],
                w_recv.at[NY - 1 + k],
                along_y(k),
            )
        )
    order = (0,) + NEAR
    for at in range(1, NZ):
        to_z[order[at]].wait_recv()
        spread(order[at])
        cross(at - 1, order[at - 1])
    cross(NZ - 1, order[NZ - 1])
    keep_weights.wait()
    to_partner.wait_send()
    for copy in to_y + to_c:
        copy.wait()
    for copy in to_x:
        copy.wait_send()
    for k in NEAR:
        to_z[k].wait_send()


def dispatch(slabs, owned):
    _, slab, features = slabs.shape
    dma = pltpu.SemaphoreType.DMA
    return pl.pallas_call(
        dispatch_kernel,
        out_shape=(
            jax.ShapeDtypeStruct((2, 2, NZ, slab, features), jnp.bfloat16),
            jax.ShapeDtypeStruct((3, 2, owned.shape[1], features), jnp.bfloat16),
        ),
        in_specs=[HBM, HBM],
        out_specs=(HBM, HBM),
        scratch_shapes=[
            dma((NZ,)),
            dma((NZ,)),
            dma((NZ,)),
            dma((NZ,)),
            dma((2, NZ)),
            dma((2, NZ)),
            dma((2 * NY - 1,)),
            dma((2 * NY - 1,)),
            dma((2,)),
        ],
        compiler_params=pltpu.CompilerParams(collective_id=0, has_side_effects=True),
        name="dispatch",
    )(slabs, owned)


FAR = (4, 3, 5, 2, 6, 1, 7, 0)


def combine_kernel(
    terms, grads, returned, gradient,
    crossed, chip, paired, slot, from_x, block, from_y, from_y_block, given, part,
    c_send, c_recv, x_send, x_recv, z_send, z_recv, g_send, g_recv, y_send, y_recv, b_send, b_recv, t_send, t_recv, local,
):
    f32, bf16 = jnp.float32, jnp.bfloat16
    y = lax.axis_index("group")
    width = gradient.shape[2]
    half = gradient.shape[1] // 2
    low, high = pl.ds(0, half), pl.ds(half, half)

    def columns(k):
        return pl.ds(pl.multiple_of((y + k) % NY * width, width), width)

    def remote(src, dst, send, recv, peer):
        copy = pltpu.make_async_remote_copy(
            src, dst, send, recv, device_id=peer, device_id_type=MESH
        )
        copy.start()
        return copy

    greet(
        [along_z(k) for k in range(1, NZ)]
        + [along_y(k) for k in range(1, NY)]
        + [token_pair(), weight_pair(), other_core()]
    )
    to_c = {
        k: remote(terms.at[1, :, k], crossed.at[k], c_send.at[k], c_recv.at[k], other_core())
        for k in FAR
    }
    to_g = [
        remote(grads.at[m, 1, high], from_x.at[m], g_send.at[m], g_recv.at[m], weight_pair())
        for m in range(3)
    ]
    to_y = [
        remote(
            grads.at[:, :, low, columns(k)], from_y.at[k - 1], y_send.at[k], y_recv.at[k], along_y(k)
        )
        for k in range(1, NY)
    ]
    to_x, to_z, to_b, to_t = {}, {}, [], []
    for k in FAR:
        to_c[k].wait_recv()
        chip[1, k] = (terms[0, 1, k].astype(f32) + crossed[k, 1].astype(f32)).astype(bf16)
        to_x[k] = remote(chip.at[1, k], paired.at[k], x_send.at[k], x_recv.at[k], token_pair())
        chip[0, k] = (terms[0, 0, k].astype(f32) + crossed[k, 0].astype(f32)).astype(bf16)

    def back(k):
        to_x[k].wait_recv()
        slot[k] = (chip[0, k].astype(f32) + paired[k].astype(f32)).astype(bf16)
        if k:
            to_z[k] = remote(
                slot.at[k], returned.at[k], z_send.at[k], z_recv.at[k], along_z(NZ - k)
            )

    def through(m):
        to_g[m].wait_recv()
        block[m] = (grads[m, 0, high].astype(f32) + from_x[m].astype(f32)).astype(bf16)
        for k in range(1, NY):
            to_b.append(
                remote(
                    block.at[m, :, columns(k)],
                    from_y_block.at[k - 1, m],
                    b_send.at[m, k],
                    b_recv.at[m, k],
                    along_y(k),
                )
            )

    mine = columns(0)
    back(FAR[0])
    back(FAR[1])
    through(0)
    back(FAR[2])
    back(FAR[3])
    through(1)
    back(FAR[4])
    back(FAR[5])
    back(FAR[6])
    through(2)
    for copy in to_y:
        copy.wait_recv()
    for m in range(3):
        for b in (1, 0):
            total = grads[m, b, low, mine].astype(f32)
            for k in range(NY - 1):
                total = total + from_y[k, m, b].astype(f32)
            if b:
                part[m] = total.astype(bf16)
                to_t.append(
                    remote(part.at[m], given.at[m], t_send.at[m], t_recv.at[m], weight_pair())
                )
            else:
                gradient[m, low] = total
    back(FAR[7])
    keep = pltpu.make_async_copy(slot.at[0], returned.at[0], local)
    keep.start()
    for copy in to_b:
        copy.wait_recv()
    for m in range(3):
        total = block[m, :, mine].astype(f32)
        for k in range(NY - 1):
            total = total + from_y_block[k, m].astype(f32)
        gradient[m, high] = total
        to_t[m].wait_recv()
        gradient[m, low] = gradient[m, low] + given[m].astype(f32)
    keep.wait()
    for k in FAR:
        to_c[k].wait_send()
        to_x[k].wait_send()
        if k:
            to_z[k].wait()
    for copy in to_g + to_y + to_b + to_t:
        copy.wait_send()


def combine(terms, grads):
    _, _, _, slab, half_width = terms.shape
    _, _, stored, features = grads.shape
    width, half = features // NY, stored // 2
    dma = pltpu.SemaphoreType.DMA
    bf16 = jnp.bfloat16
    vmem = pl.BlockSpec(memory_space=pltpu.VMEM)
    return pl.pallas_call(
        combine_kernel,
        out_shape=(
            jax.ShapeDtypeStruct((NZ, slab, half_width), bf16),
            jax.ShapeDtypeStruct((3, stored, width), jnp.float32),
        ),
        in_specs=[vmem, vmem],
        out_specs=(HBM, vmem),
        scratch_shapes=[
            pltpu.VMEM((NZ, 2, slab, half_width), bf16),
            pltpu.VMEM((2, NZ, slab, half_width), bf16),
            pltpu.VMEM((NZ, slab, half_width), bf16),
            pltpu.VMEM((NZ, slab, half_width), bf16),
            pltpu.VMEM((3, half, features), bf16),
            pltpu.VMEM((3, half, features), bf16),
            pltpu.VMEM((NY - 1, 3, 2, half, width), bf16),
            pltpu.VMEM((NY - 1, 3, half, width), bf16),
            pltpu.VMEM((3, half, width), bf16),
            pltpu.VMEM((3, half, width), bf16),
        ]
        + [dma((NZ,))] * 6
        + [dma((3,))] * 2
        + [dma((NY,))] * 2
        + [dma((3, NY))] * 2
        + [dma((3,))] * 2
        + [dma],
        compiler_params=pltpu.CompilerParams(
            collective_id=1, has_side_effects=True, vmem_limit_bytes=48 << 20
        ),
        name="combine",
    )(terms, grads)


def shards(tokens, cotangent, routes, codes, scales, first_moment, second_moment):
    row_count, features = tokens.shape
    stored, width = codes.shape[1:]
    y, z, _, _ = place()
    owned_full = codes.astype(jnp.float32) * jnp.repeat(scales, QB, axis=2)
    owned = owned_full.astype(jnp.bfloat16)

    route_ids = routes[:, 0]
    matches = route_ids[:, None] == jnp.arange(NZ, dtype=jnp.int32)[None, :]
    counted = matches.astype(jnp.int32)
    earlier = jnp.cumsum(counted, axis=0) - counted
    position = jnp.sum(jnp.where(matches, earlier, 0), axis=1)
    ahead = (route_ids - z + NZ) % NZ
    row_range = jnp.arange(row_count, dtype=jnp.int32)
    slab_range = jnp.arange(NZ * SLAB, dtype=jnp.int32)
    packing = jnp.concatenate(
        [
            (slab_range[:, None] == (ahead * SLAB + position + half * CAP)[None, :])
            for half in (0, 1)
        ],
        axis=1,
    ).astype(jnp.bfloat16)
    both = jnp.concatenate([tokens, cotangent], axis=0)
    slabs = (
        jnp.dot(packing, both, preferred_element_type=jnp.float32)
        .astype(jnp.bfloat16)
        .reshape(NZ, SLAB, features)
    )

    rows, weights = dispatch(slabs, owned)
    units = 2 * stored
    pieces = 4 * NZ
    flat_rows = rows.reshape(pieces * SLAB, features)
    flat_weights = weights.reshape(3 * units, features)
    pre = lax.dot_general(
        flat_rows, flat_weights, (((1,), (1,)), ((), ())), preferred_element_type=jnp.float32
    ).reshape(pieces, SLAB, 3 * units)
    gate = pre[:, :CAP, :units]
    up = pre[:, :CAP, units : 2 * units]
    hidden_cot = pre[:, CAP:, 2 * units :]
    sig = jax.nn.sigmoid(gate)
    activated = gate * sig
    hidden = (activated * up).astype(jnp.bfloat16)
    gate_cot = (hidden_cot * up * sig * (1.0 + gate * (1.0 - sig))).astype(jnp.bfloat16)
    up_cot = (hidden_cot * activated).astype(jnp.bfloat16)
    cots = jnp.concatenate([gate_cot, up_cot], axis=2)
    blank = jnp.zeros_like(cots)
    mixed = jnp.concatenate(
        [
            jnp.concatenate([cots, jnp.zeros_like(hidden)], axis=2),
            jnp.concatenate([blank, hidden], axis=2),
        ],
        axis=1,
    ).reshape(pieces * SLAB, 3 * units)
    grads = (
        lax.dot_general(
            mixed, flat_rows, (((0,), (0,)), ((), ())), preferred_element_type=jnp.float32
        )
        .astype(jnp.bfloat16)
        .reshape(3, 2, stored, features)
    )
    half_width = features // 2
    spread = jnp.concatenate(
        [
            jnp.concatenate([cots, blank], axis=2),
            jnp.concatenate([blank, cots], axis=2),
        ],
        axis=1,
    ).reshape(pieces * SLAB, 4 * units)
    in_weights = flat_weights[: 2 * units]
    stacked = jnp.concatenate([in_weights[:, :half_width], in_weights[:, half_width:]], axis=0)
    terms = (
        jnp.dot(spread, stacked, preferred_element_type=jnp.float32)
        .astype(jnp.bfloat16)
        .reshape(2, 2, NZ, SLAB, half_width)
    )

    returned, gradient = combine(terms, grads)
    flat_returned = returned.reshape(NZ * SLAB, half_width)
    grad_tokens = jnp.concatenate(
        [
            jnp.dot(
                ((ahead * SLAB + position + half * CAP)[:, None] == slab_range[None, :]).astype(
                    jnp.bfloat16
                ),
                flat_returned,
                preferred_element_type=jnp.float32,
            ).astype(jnp.bfloat16)
            for half in (0, 1)
        ],
        axis=1,
    )
    new_first = BETA_ONE * first_moment + (1.0 - BETA_ONE) * gradient
    new_second = BETA_TWO * second_moment + (1.0 - BETA_TWO) * gradient * gradient
    first_fix = 1.0 - BETA_ONE**STEP_COUNT
    second_fix = 1.0 - BETA_TWO**STEP_COUNT
    new_weights = owned_full - LEARNING_RATE * (new_first / first_fix) / (
        jnp.sqrt(new_second / second_fix) + ADAM_EPS
    )
    return (grad_tokens, new_weights, new_first, new_second)


def solution(mesh):
    stored = P(None, "dev", "group")
    spread = P(("group", "dev"), None)
    return jax.shard_map(
        shards,
        mesh=mesh,
        in_specs=(spread, spread, spread, stored, stored, stored, stored),
        out_specs=(spread, stored, stored, stored),
        check_vma=False,
    )
```

```python
import jax
import jax.numpy as jnp
from jax import lax
from jax.experimental import pallas as pl
from jax.experimental.pallas import tpu as pltpu
from jax.sharding import PartitionSpec as P

MESH = pl.DeviceIdType.MESH
QB = 128
NZ, NX, NY = 8, 4, 4
CAP = 20
MAIN, REST = 16, 4
PARTS = 4
ROWS = 4 * CAP
ORDER = (0, 1, 7, 2, 6, 3, 5, 4)
HBM = pl.BlockSpec(memory_space=pltpu.HBM)
VMEM = pl.BlockSpec(memory_space=pltpu.VMEM)

BETA_ONE = 0.9
BETA_TWO = 0.999
LEARNING_RATE = 0.01
ADAM_EPS = 1e-08
STEP_COUNT = 10

f32, bf16 = jnp.float32, jnp.bfloat16


def place():
    dev = lax.axis_index("dev")
    return lax.axis_index("group"), dev // 8, (dev // 2) % 4, dev % 2


def device(y, z, x, c):
    return (y, (z * NX + x) * 2 + c)


def along_z(k):
    y, z, x, c = place()
    return device(y, (z + k) % NZ, x, c)


def along_y(k):
    y, z, x, c = place()
    return device((y + k) % NY, z, x, c)


def token_pair():
    y, z, x, c = place()
    return device(y, z, x + 1 - 2 * (x % 2), c)


def weight_pair():
    y, z, x, c = place()
    return device(y, z, 3 - x, c)


def other_core():
    y, z, x, c = place()
    return device(y, z, x, 1 - c)


def greet(peers):
    barrier = pltpu.get_barrier_semaphore()
    for peer in peers:
        pl.semaphore_signal(barrier, inc=1, device_id=peer, device_id_type=MESH)
    pl.semaphore_wait(barrier, len(peers))


def remote(src, dst, send, recv, peer):
    copy = pltpu.make_async_remote_copy(src, dst, send, recv, device_id=peer, device_id_type=MESH)
    copy.start()
    return copy


def quarter_rows(part, rows_first):
    shape = (4 * MAIN, MAIN) if rows_first else (MAIN, 4 * MAIN)
    row = lax.broadcasted_iota(jnp.int32, shape, 0 if rows_first else 1)
    slot = lax.broadcasted_iota(jnp.int32, shape, 1 if rows_first else 0)
    source, inner = slot // REST, slot % REST
    return jnp.where(row == source * MAIN + part * REST + inner, 1.0, 0.0).astype(bf16)


def expert_kernel(
    slabs, owned, returned, gradient,
    inbound, weights, pre, signals, terms, rest, grads, crossed, paired,
    from_x, block, from_y, from_y_block, part, given,
    z_send, z_recv, x_send, x_recv, c_send, c_recv, w_send, w_recv,
    e_send, e_recv, p_send, p_recv, r_send, r_recv,
    g_send, g_recv, y_send, y_recv, b_send, b_recv, t_send, t_recv, local,
):
    y = lax.axis_index("group")
    stored, width = owned.shape[1:]
    features = weights.shape[3]
    units = 2 * stored
    half = stored // 2
    low, high = pl.ds(0, half), pl.ds(half, half)

    def columns(k):
        return pl.ds(pl.multiple_of((y + k) % NY * width, width), width)

    mine = columns(0)

    def source_rows(number):
        return pl.ds(number * MAIN, MAIN)

    greet(
        [along_z(k) for k in range(1, NZ)]
        + [along_y(k) for k in range(1, NY)]
        + [token_pair(), weight_pair(), other_core()]
    )

    keep_rows = pltpu.make_async_copy(
        slabs.at[0], inbound.at[:, 0, source_rows(0)], local.at[0]
    )
    keep_rows.start()
    to_z = [None]
    def launch(at):
        k = ORDER[at]
        to_z.append(
            remote(
                slabs.at[k],
                inbound.at[:, at, source_rows(0)],
                z_send.at[at],
                z_recv.at[at],
                along_z(k),
            )
        )
    for at in range(1, 5):
        launch(at)
    to_partner = remote(owned, weights.at[:, 1, :, mine], w_send.at[0], w_recv.at[0], weight_pair())
    keep_weights = pltpu.make_async_copy(owned, weights.at[:, 0, :, mine], local.at[1])
    keep_weights.start()
    to_y = [
        remote(owned, weights.at[:, 0, :, mine], w_send.at[k], w_recv.at[k], along_y(k))
        for k in range(1, NY)
    ]
    to_x, to_c = [], []

    def spread(at):
        own = inbound.at[:, at, source_rows(0)]
        to_x.append(
            remote(
                own,
                inbound.at[:, at, source_rows(1)],
                x_send.at[at],
                x_recv.at[at],
                token_pair(),
            )
        )
        to_c.append(
            [
                remote(
                    own,
                    inbound.at[:, at, source_rows(2)],
                    c_send.at[0, at],
                    c_recv.at[0, at],
                    other_core(),
                )
            ]
        )

    def cross(at):
        to_x[at].wait_recv()
        to_c[at].append(
            remote(
                inbound.at[:, at, source_rows(1)],
                inbound.at[:, at, source_rows(3)],
                c_send.at[1, at],
                c_recv.at[1, at],
                other_core(),
            )
        )

    def arrive(at):
        to_z[at].wait_recv()
        spread(at)

    def weights_on():
        to_partner.wait_recv()
        for k in range(1, NY):
            to_y.append(
                remote(
                    weights.at[:, 1, :, mine],
                    weights.at[:, 1, :, mine],
                    w_send.at[NY - 1 + k],
                    w_recv.at[NY - 1 + k],
                    along_y(k),
                )
            )

    def work(first, count):
        for at in range(first, first + count):
            for copy in to_c[at]:
                copy.wait_recv()
        rows = count * ROWS
        stretch = pl.ds(first * ROWS, rows)
        pre[:, :rows] = jnp.zeros((3, rows, units), f32)

        def project(number, carry):
            cut = pl.ds(pl.multiple_of(number * width, width), width)
            pick = quarter_rows(number, False)
            for at in range(first, first + count):
                for t in range(2):
                    inbound[t, at, 4 * MAIN :, cut] = jnp.dot(
                        pick, inbound[t, at, : 4 * MAIN, features:], preferred_element_type=f32
                    ).astype(bf16)
            for m in range(3):
                pre[m, :rows] += lax.dot_general(
                    inbound[m // 2, first : first + count, :, cut].reshape(rows, width),
                    weights[m, :, :, cut].reshape(units, width),
                    (((1,), (1,)), ((), ())),
                    preferred_element_type=f32,
                )
            return carry

        lax.fori_loop(0, PARTS, project, 0)
        gate, up, hidden_cot = pre[0, :rows], pre[1, :rows], pre[2, :rows]
        sig = jax.nn.sigmoid(gate)
        activated = gate * sig
        signals[2, stretch] = (activated * up).astype(bf16)
        signals[0, stretch] = (hidden_cot * up * sig * (1.0 + gate * (1.0 - sig))).astype(bf16)
        signals[1, stretch] = (hidden_cot * activated).astype(bf16)
        rest[...] = jnp.zeros(rest.shape, f32)

        def give_back(number, carry):
            cut = pl.ds(pl.multiple_of(number * width, width), width)
            place_rows = quarter_rows(number, True)
            term = (
                jnp.dot(
                    signals[0, stretch],
                    weights[0, :, :, cut].reshape(units, width),
                    preferred_element_type=f32,
                )
                + jnp.dot(
                    signals[1, stretch],
                    weights[1, :, :, cut].reshape(units, width),
                    preferred_element_type=f32,
                )
            ).astype(bf16)
            for i in range(count):
                one = term[i * ROWS : (i + 1) * ROWS]
                terms[first + i, :, :, cut] = one[: 4 * MAIN].reshape(4, MAIN, width)
                rest[i] += jnp.dot(place_rows, one[4 * MAIN :], preferred_element_type=f32)
            return carry

        lax.fori_loop(0, PARTS, give_back, 0)
        for i in range(count):
            terms[first + i, :, :, features:] = rest[i].astype(bf16).reshape(4, MAIN, width)
        for at in range(first, first + count):
            to_e[at] = remote(
                terms.at[at, pl.ds(2, 2)], crossed.at[at], e_send.at[at], e_recv.at[at], other_core()
            )

    to_e, to_p, to_r = {}, {}, {}

    def fold(at):
        to_e[at].wait_recv()
        for col in (1, 0):
            terms[at, col] = (terms[at, col].astype(f32) + crossed[at, col].astype(f32)).astype(bf16)
            if col:
                to_p[at] = remote(
                    terms.at[at, 1], paired.at[at], p_send.at[at], p_recv.at[at], token_pair()
                )

    def back(at):
        to_p[at].wait_recv()
        terms[at, 0] = (terms[at, 0].astype(f32) + paired[at].astype(f32)).astype(bf16)
        k = ORDER[at]
        if k:
            to_r[at] = remote(
                terms.at[at, 0], returned.at[k], r_send.at[at], r_recv.at[at], along_z(NZ - k)
            )

    to_g, to_s, to_b, to_t = [], [], [], []

    def differentiate(m):
        def columns_of(number, carry):
            cut = pl.ds(pl.multiple_of(number * (width // 2), width // 2), width // 2)
            grads[m, :, :, cut] = (
                lax.dot_general(
                    signals[m],
                    inbound[m // 2, :, :, cut].reshape(NZ * ROWS, width // 2),
                    (((0,), (0,)), ((), ())),
                    preferred_element_type=f32,
                )
                .astype(bf16)
                .reshape(2, stored, width // 2)
            )
            return carry

        lax.fori_loop(0, 2 * PARTS, columns_of, 0)
        to_g.append(
            remote(grads.at[m, 1, high], from_x.at[m], g_send.at[m], g_recv.at[m], weight_pair())
        )
        for k in range(1, NY):
            to_s.append(
                remote(
                    grads.at[m, :, low, columns(k)],
                    from_y.at[k - 1, m],
                    y_send.at[m, k],
                    y_recv.at[m, k],
                    along_y(k),
                )
            )

    def through(m):
        to_g[m].wait_recv()
        block[m] = (grads[m, 0, high].astype(f32) + from_x[m].astype(f32)).astype(bf16)
        for k in range(1, NY):
            to_b.append(
                remote(
                    block.at[m, :, columns(k)],
                    from_y_block.at[k - 1, m],
                    b_send.at[m, k],
                    b_recv.at[m, k],
                    along_y(k),
                )
            )

    def gather(m):
        for copy in to_s[m * (NY - 1) : (m + 1) * (NY - 1)]:
            copy.wait_recv()
        for b in (1, 0):
            total = grads[m, b, low, mine].astype(f32)
            for k in range(NY - 1):
                total = total + from_y[k, m, b].astype(f32)
            if b:
                part[m] = total.astype(bf16)
                to_t.append(
                    remote(part.at[m], given.at[m], t_send.at[m], t_recv.at[m], weight_pair())
                )
            else:
                gradient[m, low] = total

    def finish(m):
        for copy in to_b[m * (NY - 1) : (m + 1) * (NY - 1)]:
            copy.wait_recv()
        total = block[m, :, mine].astype(f32)
        for k in range(NY - 1):
            total = total + from_y_block[k, m].astype(f32)
        gradient[m, high] = total
        to_t[m].wait_recv()
        gradient[m, low] = gradient[m, low] + given[m].astype(f32)

    keep_rows.wait()
    spread(0)
    weights_on()
    for at in range(1, 6):
        arrive(at)
        if at + 4 < NZ:
            launch(at + 4)
        cross(at - 1)
    keep_weights.wait()
    for copy in to_y:
        copy.wait_recv()
    arrive(6)
    cross(5)
    work(0, 5)
    arrive(7)
    cross(6)
    work(5, 2)
    cross(7)
    work(7, 1)
    FAR = (7, 6, 5, 4, 3, 2, 1, 0)
    for at in FAR:
        fold(at)
    for m in range(3):
        differentiate(m)
    back(FAR[0])
    back(FAR[1])
    through(0)
    back(FAR[2])
    gather(0)
    back(FAR[3])
    through(1)
    back(FAR[4])
    gather(1)
    back(FAR[5])
    back(FAR[6])
    through(2)
    back(FAR[7])
    keep = pltpu.make_async_copy(terms.at[0, 0], returned.at[0], local.at[0])
    keep.start()
    gather(2)
    for m in range(3):
        finish(m)
    keep.wait()
    for at in range(NZ):
        to_e[at].wait_send()
        to_p[at].wait_send()
        to_x[at].wait_send()
        for copy in to_c[at]:
            copy.wait_send()
        if at:
            to_z[at].wait_send()
            to_r[at].wait()
    to_partner.wait_send()
    for copy in to_y + to_g + to_s + to_b + to_t:
        copy.wait_send()


def expert_step(slabs, owned):
    _, _, _, long = slabs.shape
    _, stored, width = owned.shape
    features = NY * width
    units, half = 2 * stored, stored // 2
    dma = pltpu.SemaphoreType.DMA
    return pl.pallas_call(
        expert_kernel,
        out_shape=(
            jax.ShapeDtypeStruct((NZ, MAIN, long), bf16),
            jax.ShapeDtypeStruct((3, stored, width), f32),
        ),
        in_specs=[HBM, HBM],
        out_specs=(HBM, VMEM),
        scratch_shapes=[
            pltpu.VMEM((2, NZ, ROWS, long), bf16),
            pltpu.VMEM((3, 2, stored, features), bf16),
            pltpu.VMEM((3, 5 * ROWS, units), f32),
            pltpu.VMEM((3, NZ * ROWS, units), bf16),
            pltpu.VMEM((NZ, 4, MAIN, long), bf16),
            pltpu.VMEM((5, 4 * MAIN, width), f32),
            pltpu.VMEM((3, 2, stored, features), bf16),
            pltpu.VMEM((NZ, 2, MAIN, long), bf16),
            pltpu.VMEM((NZ, MAIN, long), bf16),
            pltpu.VMEM((3, half, features), bf16),
            pltpu.VMEM((3, half, features), bf16),
            pltpu.VMEM((NY - 1, 3, 2, half, width), bf16),
            pltpu.VMEM((NY - 1, 3, half, width), bf16),
            pltpu.VMEM((3, half, width), bf16),
            pltpu.VMEM((3, half, width), bf16),
        ]
        + [dma((NZ,))] * 4
        + [dma((2, NZ))] * 2
        + [dma((2 * NY - 1,))] * 2
        + [dma((NZ,))] * 6
        + [dma((3,))] * 2
        + [dma((3, NY))] * 4
        + [dma((3,))] * 2
        + [dma((2,))],
        compiler_params=pltpu.CompilerParams(
            collective_id=0, has_side_effects=True, vmem_limit_bytes=60 << 20
        ),
        cost_estimate=pl.CostEstimate(flops=10 * 10**9, bytes_accessed=10**8, transcendentals=0),
        name="expert_step",
    )(slabs, owned)


def shards(tokens, cotangent, routes, codes, scales, first_moment, second_moment):
    row_count, features = tokens.shape
    stored, width = codes.shape[1:]
    _, z, _, _ = place()
    owned_full = codes.astype(f32) * jnp.repeat(scales, QB, axis=2)
    owned = owned_full.astype(bf16)

    route_ids = routes[:, 0]
    matches = route_ids[:, None] == jnp.arange(NZ, dtype=jnp.int32)[None, :]
    counted = matches.astype(jnp.int32)
    earlier = jnp.cumsum(counted, axis=0) - counted
    position = jnp.sum(jnp.where(matches, earlier, 0), axis=1)
    ahead = (route_ids - z + NZ) % NZ
    main_slot = jnp.where(position < MAIN, ahead * MAIN + position, -1)

    def rest_slot(part):
        return jnp.where(position < MAIN, -1, ahead * MAIN + part * REST + position - MAIN)

    slots = jnp.arange(NZ * MAIN, dtype=jnp.int32)

    def pack(values):
        main = jnp.dot(
            (slots[:, None] == main_slot[None, :]).astype(bf16), values, preferred_element_type=f32
        )
        chosen = jnp.concatenate(
            [slots[:, None] == rest_slot(part)[None, :] for part in range(PARTS)], axis=1
        ).astype(bf16)
        quarters = jnp.concatenate(
            [values[:, part * width : (part + 1) * width] for part in range(PARTS)], axis=0
        )
        rest = jnp.dot(chosen, quarters, preferred_element_type=f32)
        packed = jnp.concatenate([main.astype(bf16), rest.astype(bf16)], axis=1)
        return packed.reshape(NZ, MAIN, features + width)

    slabs = jnp.stack([pack(tokens), pack(cotangent)], axis=1)
    returned, gradient = expert_step(slabs, owned)
    flat = returned.reshape(NZ * MAIN, features + width)
    grad_tokens = jnp.concatenate(
        [
            jnp.dot(
                jnp.concatenate(
                    [
                        main_slot[:, None] == slots[None, :],
                        rest_slot(part)[:, None] == slots[None, :],
                    ],
                    axis=1,
                ).astype(bf16),
                jnp.concatenate(
                    [flat[:, part * width : (part + 1) * width], flat[:, features:]], axis=0
                ),
                preferred_element_type=f32,
            ).astype(bf16)
            for part in range(PARTS)
        ],
        axis=1,
    )
    new_first = BETA_ONE * first_moment + (1.0 - BETA_ONE) * gradient
    new_second = BETA_TWO * second_moment + (1.0 - BETA_TWO) * gradient * gradient
    first_fix = 1.0 - BETA_ONE**STEP_COUNT
    second_fix = 1.0 - BETA_TWO**STEP_COUNT
    new_weights = owned_full - LEARNING_RATE * (new_first / first_fix) / (
        jnp.sqrt(new_second / second_fix) + ADAM_EPS
    )
    return (grad_tokens, new_weights, new_first, new_second)


def solution(mesh):
    stored = P(None, "dev", "group")
    spread = P(("group", "dev"), None)
    return jax.shard_map(
        shards,
        mesh=mesh,
        in_specs=(spread, spread, spread, stored, stored, stored, stored),
        out_specs=(spread, stored, stored, stored),
        check_vma=False,
    )
```

```python
import jax
import jax.numpy as jnp
from jax import lax
from jax.experimental import pallas as pl
from jax.experimental.pallas import tpu as pltpu
from jax.sharding import PartitionSpec as P

MESH = pl.DeviceIdType.MESH
QB = 128
NZ, NX, NY = 8, 4, 4
CAP = 20
MAIN, REST = 16, 4
PARTS = 4
ROWS = 4 * CAP
ORDER = (0, 1, 7, 2, 6, 3, 5, 4)
HBM = pl.BlockSpec(memory_space=pltpu.HBM)
VMEM = pl.BlockSpec(memory_space=pltpu.VMEM)

BETA_ONE = 0.9
BETA_TWO = 0.999
LEARNING_RATE = 0.01
ADAM_EPS = 1e-08
STEP_COUNT = 10

f32, bf16 = jnp.float32, jnp.bfloat16


def place():
    dev = lax.axis_index("dev")
    return lax.axis_index("group"), dev // 8, (dev // 2) % 4, dev % 2


def device(y, z, x, c):
    return (y, (z * NX + x) * 2 + c)


def along_z(k):
    y, z, x, c = place()
    return device(y, (z + k) % NZ, x, c)


def along_y(k):
    y, z, x, c = place()
    return device((y + k) % NY, z, x, c)


def token_pair():
    y, z, x, c = place()
    return device(y, z, x + 1 - 2 * (x % 2), c)


def weight_pair():
    y, z, x, c = place()
    return device(y, z, 3 - x, c)


def other_core():
    y, z, x, c = place()
    return device(y, z, x, 1 - c)


def remote(src, dst, send, recv, peer):
    copy = pltpu.make_async_remote_copy(src, dst, send, recv, device_id=peer, device_id_type=MESH)
    copy.start()
    return copy


def quarter_rows(part, rows_first):
    shape = (4 * MAIN, MAIN) if rows_first else (MAIN, 4 * MAIN)
    row = lax.broadcasted_iota(jnp.int32, shape, 0 if rows_first else 1)
    slot = lax.broadcasted_iota(jnp.int32, shape, 1 if rows_first else 0)
    source, inner = slot // REST, slot % REST
    return jnp.where(row == source * MAIN + part * REST + inner, 1.0, 0.0).astype(bf16)


def expert_kernel(
    tokens, cotangent, routes, codes, scales, token_grads, gradient,
    slabs, owned, returned, picks, unpicks, inbound, weights, pre, signals, terms, rest, grads, crossed, paired,
    from_x, block, from_y, from_y_block, part, given,
    z_send, z_recv, x_send, x_recv, c_send, c_recv, w_send, w_recv,
    e_send, e_recv, p_send, p_recv, r_send, r_recv,
    g_send, g_recv, y_send, y_recv, b_send, b_recv, t_send, t_recv, local, load,
):
    y = lax.axis_index("group")
    stored, width = owned.shape[1:]
    features = weights.shape[3]
    tail = pl.ds(features, width)
    units = 2 * stored
    half = stored // 2
    low, high = pl.ds(0, half), pl.ds(half, half)

    def columns(k):
        return pl.ds(pl.multiple_of((y + k) % NY * width, width), width)

    mine = columns(0)

    def source_rows(number):
        return pl.ds(number * MAIN, MAIN)

    peers = (
        [along_z(k) for k in range(1, NZ)]
        + [along_y(k) for k in range(1, NY)]
        + [token_pair(), weight_pair(), other_core()]
    )
    barrier = pltpu.get_barrier_semaphore()
    for peer in peers:
        pl.semaphore_signal(barrier, inc=1, device_id=peer, device_id_type=MESH)

    loads = []
    for t, source in enumerate((tokens, cotangent)):
        loads.append(
            pltpu.make_async_copy(
                source, terms.at[pl.ds(2 * t, 2), :, :, pl.ds(0, features)], load.at[t]
            )
        )
        loads[t].start()
    for b in range(scales.shape[2]):
        cut = pl.ds(b * QB, QB)
        owned[:, :, cut] = (codes[:, :, cut].astype(f32) * scales[:, :, b : b + 1]).astype(bf16)

    count = routes.shape[1]
    _, z, _, _ = place()
    row_range = lax.broadcasted_iota(jnp.int32, (count, count), 0)
    column_range = lax.broadcasted_iota(jnp.int32, (count, count), 1)
    before = jnp.where(row_range < column_range, 1.0, 0.0).astype(bf16)
    matches = lax.broadcasted_iota(jnp.int32, (MAIN, count), 0) == routes[...]
    earlier = jnp.dot(
        jnp.where(matches, 1.0, 0.0).astype(bf16), before, preferred_element_type=f32
    )
    position = jnp.sum(jnp.where(matches, earlier, 0.0), axis=0, keepdims=True).astype(jnp.int32)
    first_slot = (routes[...] - z + NZ) % NZ * MAIN
    in_main = position < MAIN
    for number in range(PARTS + 1):
        if number < PARTS:
            slot = jnp.where(in_main, -1, first_slot + number * REST + position - MAIN)
        else:
            slot = jnp.where(in_main, first_slot + position, -1)
        pick = jnp.where(row_range == slot, 1.0, 0.0)
        picks[number] = pick.astype(bf16)
        unpicks[number] = pick.T.astype(bf16)

    pl.semaphore_wait(barrier, len(peers))

    to_partner = remote(owned, weights.at[:, 1, :, mine], w_send.at[0], w_recv.at[0], weight_pair())
    keep_weights = pltpu.make_async_copy(owned, weights.at[:, 0, :, mine], local.at[1])
    keep_weights.start()
    to_y = [
        remote(owned, weights.at[:, 0, :, mine], w_send.at[k], w_recv.at[k], along_y(k))
        for k in range(1, NY)
    ]
    for t in range(2):
        loads[t].wait()

        def pack(number, carry):
            cut = pl.ds(pl.multiple_of(number * width, width), width)
            values = terms[2 * t : 2 * t + 2, :, :, cut].reshape(count, width)
            slabs[:, t, :, cut] = (
                jnp.dot(picks[PARTS], values, preferred_element_type=f32)
                .astype(bf16)
                .reshape(NZ, MAIN, width)
            )
            left = jnp.dot(picks[number], values, preferred_element_type=f32)
            slabs[:, t, :, tail] = slabs[:, t, :, tail] + left.astype(bf16).reshape(NZ, MAIN, width)
            return carry

        slabs[:, t, :, tail] = jnp.zeros((NZ, MAIN, width), bf16)
        lax.fori_loop(0, PARTS, pack, 0)
    keep_rows = pltpu.make_async_copy(
        slabs.at[0], inbound.at[:, 0, source_rows(0)], local.at[0]
    )
    keep_rows.start()
    to_z = [None]
    def launch(at):
        k = ORDER[at]
        to_z.append(
            remote(
                slabs.at[k],
                inbound.at[:, at, source_rows(0)],
                z_send.at[at],
                z_recv.at[at],
                along_z(k),
            )
        )
    for at in range(1, 5):
        launch(at)
    to_x, to_c = [], []

    def spread(at):
        own = inbound.at[:, at, source_rows(0)]
        to_x.append(
            remote(
                own,
                inbound.at[:, at, source_rows(1)],
                x_send.at[at],
                x_recv.at[at],
                token_pair(),
            )
        )
        to_c.append(
            [
                remote(
                    own,
                    inbound.at[:, at, source_rows(2)],
                    c_send.at[0, at],
                    c_recv.at[0, at],
                    other_core(),
                )
            ]
        )

    def cross(at):
        to_x[at].wait_recv()
        to_c[at].append(
            remote(
                inbound.at[:, at, source_rows(1)],
                inbound.at[:, at, source_rows(3)],
                c_send.at[1, at],
                c_recv.at[1, at],
                other_core(),
            )
        )

    def arrive(at):
        to_z[at].wait_recv()
        spread(at)

    def weights_on():
        to_partner.wait_recv()
        for k in range(1, NY):
            to_y.append(
                remote(
                    weights.at[:, 1, :, mine],
                    weights.at[:, 1, :, mine],
                    w_send.at[NY - 1 + k],
                    w_recv.at[NY - 1 + k],
                    along_y(k),
                )
            )

    def unpack_rest(first, count):
        for at in range(first, first + count):
            for copy in to_c[at]:
                copy.wait_recv()

        def unpack(number, carry):
            cut = pl.ds(pl.multiple_of(number * width, width), width)
            pick = quarter_rows(number, False)
            for at in range(first, first + count):
                for t in range(2):
                    inbound[t, at, 4 * MAIN :, cut] = jnp.dot(
                        pick, inbound[t, at, : 4 * MAIN, features:], preferred_element_type=f32
                    ).astype(bf16)
            return carry

        lax.fori_loop(0, PARTS, unpack, 0)

    def project(first, count, turns):
        rows = count * ROWS
        stretch = pl.ds(first * ROWS, rows)
        for k in turns:
            cut = columns(NY - k)
            for m in range(3):
                term = lax.dot_general(
                    inbound[m // 2, first : first + count, :, cut].reshape(rows, width),
                    weights[m, :, :, cut].reshape(units, width),
                    (((1,), (1,)), ((), ())),
                    preferred_element_type=f32,
                )
                if k == 0:
                    pre[m, stretch] = term
                else:
                    pre[m, stretch] += term

    def activate(first, count):
        stretch = pl.ds(first * ROWS, count * ROWS)
        gate, up, hidden_cot = pre[0, stretch], pre[1, stretch], pre[2, stretch]
        sig = jax.nn.sigmoid(gate)
        activated = gate * sig
        signals[2, stretch] = (activated * up).astype(bf16)
        signals[0, stretch] = (hidden_cot * up * sig * (1.0 + gate * (1.0 - sig))).astype(bf16)
        signals[1, stretch] = (hidden_cot * activated).astype(bf16)

    def give_back(first, count, low_part, high_part):
        stretch = pl.ds(first * ROWS, count * ROWS)

        def one_part(number, carry):
            cut = pl.ds(pl.multiple_of(number * width, width), width)
            place_rows = quarter_rows(number, True)
            term = (
                jnp.dot(
                    signals[0, stretch],
                    weights[0, :, :, cut].reshape(units, width),
                    preferred_element_type=f32,
                )
                + jnp.dot(
                    signals[1, stretch],
                    weights[1, :, :, cut].reshape(units, width),
                    preferred_element_type=f32,
                )
            ).astype(bf16)
            for i in range(count):
                one = term[i * ROWS : (i + 1) * ROWS]
                terms[first + i, :, :, cut] = one[: 4 * MAIN].reshape(4, MAIN, width)
                rest[i] += jnp.dot(place_rows, one[4 * MAIN :], preferred_element_type=f32)
            return carry

        if low_part == 0:
            rest[:count] = jnp.zeros((count,) + rest.shape[1:], f32)
        lax.fori_loop(low_part, high_part, one_part, 0)
        if high_part == PARTS:
            for i in range(count):
                terms[first + i, :, :, features:] = rest[i].astype(bf16).reshape(4, MAIN, width)
            for at in range(first, first + count):
                to_e[at] = remote(
                    terms.at[at, pl.ds(2, 2)],
                    crossed.at[at],
                    e_send.at[at],
                    e_recv.at[at],
                    other_core(),
                )

    def weights_of(k):
        if k:
            to_y[k - 1].wait_recv()
            to_y[NY - 2 + k].wait_recv()
        else:
            keep_weights.wait()

    to_e, to_p, to_r = {}, {}, {}

    def fold(at):
        to_e[at].wait_recv()
        for col in (1, 0):
            terms[at, col] = (terms[at, col].astype(f32) + crossed[at, col].astype(f32)).astype(bf16)
            if col:
                to_p[at] = remote(
                    terms.at[at, 1], paired.at[at], p_send.at[at], p_recv.at[at], token_pair()
                )

    def back(at):
        to_p[at].wait_recv()
        total = (terms[at, 0].astype(f32) + paired[at].astype(f32)).astype(bf16)
        k = ORDER[at]
        if k == 0:
            returned[0] = total
        else:
            terms[at, 0] = total
            to_r[at] = remote(
                terms.at[at, 0], returned.at[k], r_send.at[at], r_recv.at[at], along_z(NZ - k)
            )

    to_g, to_s, to_b, to_t = [], [], [], []

    def differentiate(m):
        def columns_of(number, carry):
            cut = pl.ds(pl.multiple_of(number * (width // 2), width // 2), width // 2)
            grads[m, :, :, cut] = (
                lax.dot_general(
                    signals[m],
                    inbound[m // 2, :, :, cut].reshape(NZ * ROWS, width // 2),
                    (((0,), (0,)), ((), ())),
                    preferred_element_type=f32,
                )
                .astype(bf16)
                .reshape(2, stored, width // 2)
            )
            return carry

        lax.fori_loop(0, 2 * PARTS, columns_of, 0)
        to_g.append(
            remote(grads.at[m, 1, high], from_x.at[m], g_send.at[m], g_recv.at[m], weight_pair())
        )
        for k in range(1, NY):
            to_s.append(
                remote(
                    grads.at[m, :, low, columns(k)],
                    from_y.at[k - 1, m],
                    y_send.at[m, k],
                    y_recv.at[m, k],
                    along_y(k),
                )
            )

    def through(m):
        to_g[m].wait_recv()
        block[m] = (grads[m, 0, high].astype(f32) + from_x[m].astype(f32)).astype(bf16)
        for k in range(1, NY):
            to_b.append(
                remote(
                    block.at[m, :, columns(k)],
                    from_y_block.at[k - 1, m],
                    b_send.at[m, k],
                    b_recv.at[m, k],
                    along_y(k),
                )
            )

    def gather(m):
        for copy in to_s[m * (NY - 1) : (m + 1) * (NY - 1)]:
            copy.wait_recv()
        for b in (1, 0):
            total = grads[m, b, low, mine].astype(f32)
            for k in range(NY - 1):
                total = total + from_y[k, m, b].astype(f32)
            if b:
                part[m] = total.astype(bf16)
                to_t.append(
                    remote(part.at[m], given.at[m], t_send.at[m], t_recv.at[m], weight_pair())
                )
            else:
                gradient[m, low] = total

    def finish(m):
        for copy in to_b[m * (NY - 1) : (m + 1) * (NY - 1)]:
            copy.wait_recv()
        total = block[m, :, mine].astype(f32)
        for k in range(NY - 1):
            total = total + from_y_block[k, m].astype(f32)
        gradient[m, high] = total
        to_t[m].wait_recv()
        gradient[m, low] = gradient[m, low] + given[m].astype(f32)

    keep_rows.wait()
    spread(0)
    arrive(1)
    launch(5)
    cross(0)
    arrive(2)
    launch(6)
    weights_on()
    cross(1)
    cross(2)
    arrive(3)
    launch(7)
    arrive(4)
    cross(3)
    cross(4)
    unpack_rest(0, 5)
    weights_of(0)
    project(0, 5, (0,))
    weights_of(1)
    project(0, 5, (1,))
    arrive(5)
    weights_of(3)
    project(0, 5, (3,))
    arrive(6)
    cross(5)
    weights_of(2)
    project(0, 5, (2,))
    activate(0, 5)
    cross(6)
    give_back(0, 5, 0, 2)
    arrive(7)
    give_back(0, 5, 2, 4)
    unpack_rest(5, 2)
    project(5, 2, (0, 1, 3, 2))
    activate(5, 2)
    give_back(5, 2, 0, 4)
    cross(7)
    unpack_rest(7, 1)
    project(7, 1, (0, 1, 3, 2))
    activate(7, 1)
    FAR = (6, 5, 7, 4, 3, 2, 1, 0)
    for at in (6, 5):
        fold(at)
    for m in range(3):
        differentiate(m)
    give_back(7, 1, 0, 4)
    for at in FAR[2:]:
        fold(at)
    back(FAR[0])
    back(FAR[1])
    through(0)
    back(FAR[2])
    gather(0)
    back(FAR[3])
    through(1)
    back(FAR[4])
    gather(1)
    back(FAR[5])
    back(FAR[6])
    through(2)
    back(FAR[7])
    gather(2)
    for at in range(1, NZ):
        to_r[at].wait_recv()

    def unpack_tokens(number, carry):
        cut = pl.ds(pl.multiple_of(number * width, width), width)
        token_grads[:, cut] = (
            jnp.dot(
                unpicks[PARTS],
                returned[:, :, cut].reshape(count, width),
                preferred_element_type=f32,
            )
            + jnp.dot(
                unpicks[number],
                returned[:, :, tail].reshape(count, width),
                preferred_element_type=f32,
            )
        ).astype(bf16)
        return carry

    lax.fori_loop(0, PARTS, unpack_tokens, 0)
    for m in range(3):
        finish(m)
    for at in range(NZ):
        to_e[at].wait_send()
        to_p[at].wait_send()
        to_x[at].wait_send()
        for copy in to_c[at]:
            copy.wait_send()
        if at:
            to_z[at].wait_send()
            to_r[at].wait_send()
    to_partner.wait_send()
    for copy in to_y + to_g + to_s + to_b + to_t:
        copy.wait_send()


def expert_step(tokens, cotangent, routes, codes, scales):
    count, features = tokens.shape
    _, stored, width = codes.shape
    long = features + width
    units, half = 2 * stored, stored // 2
    dma = pltpu.SemaphoreType.DMA
    return pl.pallas_call(
        expert_kernel,
        out_shape=(
            jax.ShapeDtypeStruct((count, features), bf16),
            jax.ShapeDtypeStruct((3, stored, width), f32),
        ),
        in_specs=[HBM, HBM, VMEM, VMEM, VMEM],
        out_specs=(VMEM, VMEM),
        scratch_shapes=[
            pltpu.VMEM((NZ, 2, MAIN, long), bf16),
            pltpu.VMEM((3, stored, width), bf16),
            pltpu.VMEM((NZ, MAIN, long), bf16),
            pltpu.VMEM((PARTS + 1, count, count), bf16),
            pltpu.VMEM((PARTS + 1, count, count), bf16),
            pltpu.VMEM((2, NZ, ROWS, long), bf16),
            pltpu.VMEM((3, 2, stored, features), bf16),
            pltpu.VMEM((3, NZ * ROWS, units), f32),
            pltpu.VMEM((3, NZ * ROWS, units), bf16),
            pltpu.VMEM((NZ, 4, MAIN, long), bf16),
            pltpu.VMEM((5, 4 * MAIN, width), f32),
            pltpu.VMEM((3, 2, stored, features), bf16),
            pltpu.VMEM((NZ, 2, MAIN, long), bf16),
            pltpu.VMEM((NZ, MAIN, long), bf16),
            pltpu.VMEM((3, half, features), bf16),
            pltpu.VMEM((3, half, features), bf16),
            pltpu.VMEM((NY - 1, 3, 2, half, width), bf16),
            pltpu.VMEM((NY - 1, 3, half, width), bf16),
            pltpu.VMEM((3, half, width), bf16),
            pltpu.VMEM((3, half, width), bf16),
        ]
        + [dma((NZ,))] * 4
        + [dma((2, NZ))] * 2
        + [dma((2 * NY - 1,))] * 2
        + [dma((NZ,))] * 6
        + [dma((3,))] * 2
        + [dma((3, NY))] * 4
        + [dma((3,))] * 2
        + [dma((2,))] * 2,
        compiler_params=pltpu.CompilerParams(
            collective_id=0, has_side_effects=True, vmem_limit_bytes=62 << 20
        ),
        cost_estimate=pl.CostEstimate(flops=10 * 10**9, bytes_accessed=10**8, transcendentals=0),
        name="expert_step",
    )(
        tokens.reshape(2, 4, MAIN, features),
        cotangent.reshape(2, 4, MAIN, features),
        routes.reshape(1, count),
        codes,
        scales,
    )


def shards(tokens, cotangent, routes, codes, scales, first_moment, second_moment):
    owned_full = codes.astype(f32) * jnp.repeat(scales, QB, axis=2)
    grad_tokens, gradient = expert_step(tokens, cotangent, routes, codes, scales)
    new_first = BETA_ONE * first_moment + (1.0 - BETA_ONE) * gradient
    new_second = BETA_TWO * second_moment + (1.0 - BETA_TWO) * gradient * gradient
    first_fix = 1.0 - BETA_ONE**STEP_COUNT
    second_fix = 1.0 - BETA_TWO**STEP_COUNT
    new_weights = owned_full - LEARNING_RATE * (new_first / first_fix) / (
        jnp.sqrt(new_second / second_fix) + ADAM_EPS
    )
    return (grad_tokens, new_weights, new_first, new_second)


def solution(mesh):
    stored = P(None, "dev", "group")
    spread = P(("group", "dev"), None)
    return jax.shard_map(
        shards,
        mesh=mesh,
        in_specs=(spread, spread, spread, stored, stored, stored, stored),
        out_specs=(spread, stored, stored, stored),
        check_vma=False,
    )
```

```python
import jax
import jax.numpy as jnp
from jax import lax
from jax.experimental import pallas as pl
from jax.experimental.pallas import tpu as pltpu
from jax.sharding import PartitionSpec as P

MESH = pl.DeviceIdType.MESH
QB = 128
NZ, NX, NY = 8, 4, 4
CAP = 20
MAIN, REST = 16, 4
PARTS = 4
ROWS = 4 * CAP
NEXT = (1, 3)
ORDER = (0, 1, 7, 2, 6, 3, 5, 4)
HBM = pl.BlockSpec(memory_space=pltpu.HBM)
VMEM = pl.BlockSpec(memory_space=pltpu.VMEM)

BETA_ONE = 0.9
BETA_TWO = 0.999
LEARNING_RATE = 0.01
ADAM_EPS = 1e-08
STEP_COUNT = 10

f32, bf16 = jnp.float32, jnp.bfloat16


def place():
    dev = lax.axis_index("dev")
    return lax.axis_index("group"), dev // 8, (dev // 2) % 4, dev % 2


def device(y, z, x, c):
    return (y, (z * NX + x) * 2 + c)


def along_z(k):
    y, z, x, c = place()
    return device(y, (z + k) % NZ, x, c)


def along_y(k):
    y, z, x, c = place()
    return device((y + k) % NY, z, x, c)


def token_pair():
    y, z, x, c = place()
    return device(y, z, x + 1 - 2 * (x % 2), c)


def weight_pair():
    y, z, x, c = place()
    return device(y, z, 3 - x, c)


def other_core():
    y, z, x, c = place()
    return device(y, z, x, 1 - c)


def remote(src, dst, send, recv, peer):
    copy = pltpu.make_async_remote_copy(src, dst, send, recv, device_id=peer, device_id_type=MESH)
    copy.start()
    return copy


def quarter_rows(part, rows_first):
    shape = (4 * MAIN, MAIN) if rows_first else (MAIN, 4 * MAIN)
    row = lax.broadcasted_iota(jnp.int32, shape, 0 if rows_first else 1)
    slot = lax.broadcasted_iota(jnp.int32, shape, 1 if rows_first else 0)
    source, inner = slot // REST, slot % REST
    return jnp.where(row == source * MAIN + part * REST + inner, 1.0, 0.0).astype(bf16)


def expert_kernel(
    tokens, cotangent, routes, codes, scales, token_grads, gradient, full,
    slabs, owned, returned, picks, unpicks, inbound, weights, pre, signals, terms, rest, grads, crossed, paired,
    from_x, block, far_y, far_block, from_y, from_y_block, part, given,
    z_send, z_recv, x_send, x_recv, c_send, c_recv, w_send, w_recv,
    e_send, e_recv, p_send, p_recv, r_send, r_recv,
    g_send, g_recv, f_send, f_recv, h_send, h_recv, y_send, y_recv, b_send, b_recv, t_send, t_recv, local, load,
):
    y = lax.axis_index("group")
    stored, width = owned.shape[1:]
    features = weights.shape[3]
    tail = pl.ds(features, width)
    units = 2 * stored
    half = stored // 2
    low, high = pl.ds(0, half), pl.ds(half, half)

    def columns(k):
        return pl.ds(pl.multiple_of((y + k) % NY * width, width), width)

    mine = columns(0)

    def source_rows(number):
        return pl.ds(number * MAIN, MAIN)

    peers = (
        [along_z(k) for k in range(1, NZ)]
        + [along_y(k) for k in range(1, NY)]
        + [token_pair(), weight_pair(), other_core()]
    )
    barrier = pltpu.get_barrier_semaphore()
    for peer in peers:
        pl.semaphore_signal(barrier, inc=1, device_id=peer, device_id_type=MESH)

    loads = []
    for t, source in enumerate((tokens, cotangent)):
        loads.append(
            pltpu.make_async_copy(
                source, terms.at[pl.ds(2 * t, 2), :, :, pl.ds(0, features)], load.at[t]
            )
        )
        loads[t].start()
    for m in range(3):
        columned = scales[m].T
        for b in range(scales.shape[1]):
            cut = pl.ds(b * QB, QB)
            full[m, :, cut] = codes[m, :, cut].astype(f32) * columned[:, b : b + 1]
            owned[m, :, cut] = full[m, :, cut].astype(bf16)

    count = routes.shape[1]
    _, z, _, _ = place()
    row_range = lax.broadcasted_iota(jnp.int32, (count, count), 0)
    column_range = lax.broadcasted_iota(jnp.int32, (count, count), 1)
    before = jnp.where(row_range < column_range, 1.0, 0.0).astype(bf16)
    matches = lax.broadcasted_iota(jnp.int32, (MAIN, count), 0) == routes[...]
    earlier = jnp.dot(
        jnp.where(matches, 1.0, 0.0).astype(bf16), before, preferred_element_type=f32
    )
    position = jnp.sum(jnp.where(matches, earlier, 0.0), axis=0, keepdims=True).astype(jnp.int32)
    first_slot = (routes[...] - z + NZ) % NZ * MAIN
    in_main = position < MAIN
    main = jnp.where(row_range == jnp.where(in_main, first_slot + position, -1), 1.0, 0.0)
    unpicks[PARTS] = main.T.astype(bf16)
    for number in range(PARTS):
        slot = jnp.where(in_main, -1, first_slot + number * REST + position - MAIN)
        pick = jnp.where(row_range == slot, 1.0, 0.0)
        picks[number, :count] = main.astype(bf16)
        picks[number, count:] = pick.astype(bf16)
        unpicks[number] = pick.T.astype(bf16)

    pl.semaphore_wait(barrier, len(peers))

    to_partner = remote(
        owned, weights.at[:, 1, :, mine], w_send.at[2 * NY], w_recv.at[2 * NY], weight_pair()
    )
    keep_weights = pltpu.make_async_copy(owned, weights.at[:, 0, :, mine], local.at[1])
    keep_weights.start()
    to_y = {
        (0, k): remote(owned, weights.at[:, 0, :, mine], w_send.at[k], w_recv.at[k], along_y(k))
        for k in NEXT
    }
    for t in range(2):
        loads[t].wait()

        def pack(number, carry):
            cut = pl.ds(pl.multiple_of(number * width, width), width)
            values = terms[2 * t : 2 * t + 2, :, :, cut].reshape(count, width)
            packed = jnp.dot(
                picks[number], values, preferred_element_type=f32
            ).astype(bf16)
            slabs[:, t, :, cut] = packed[:count].reshape(NZ, MAIN, width)
            slabs[:, t, :, tail] = slabs[:, t, :, tail] + packed[count:].reshape(NZ, MAIN, width)
            return carry

        slabs[:, t, :, tail] = jnp.zeros((NZ, MAIN, width), bf16)
        lax.fori_loop(0, PARTS, pack, 0)
    keep_rows = pltpu.make_async_copy(
        slabs.at[0], inbound.at[:, 0, source_rows(0)], local.at[0]
    )
    keep_rows.start()
    to_z = [None]
    def launch(at):
        k = ORDER[at]
        to_z.append(
            remote(
                slabs.at[k],
                inbound.at[:, at, source_rows(0)],
                z_send.at[at],
                z_recv.at[at],
                along_z(k),
            )
        )
    for at in range(1, 5):
        launch(at)
    to_x, to_c = [], []

    def spread(at):
        own = inbound.at[:, at, source_rows(0)]
        to_x.append(
            remote(
                own,
                inbound.at[:, at, source_rows(1)],
                x_send.at[at],
                x_recv.at[at],
                token_pair(),
            )
        )
        to_c.append(
            [
                remote(
                    own,
                    inbound.at[:, at, source_rows(2)],
                    c_send.at[0, at],
                    c_recv.at[0, at],
                    other_core(),
                )
            ]
        )

    def cross(at):
        to_x[at].wait_recv()
        to_c[at].append(
            remote(
                inbound.at[:, at, source_rows(1)],
                inbound.at[:, at, source_rows(3)],
                c_send.at[1, at],
                c_recv.at[1, at],
                other_core(),
            )
        )

    def arrive(at):
        to_z[at].wait_recv()
        spread(at)

    def weights_on():
        to_partner.wait_recv()
        for k in NEXT:
            to_y[1, k] = remote(
                weights.at[:, 1, :, mine],
                weights.at[:, 1, :, mine],
                w_send.at[NY + k],
                w_recv.at[NY + k],
                along_y(k),
            )

    def relay(b):
        for way, k in enumerate(NEXT):
            to_y[b, k].wait_recv()
            passed = weights.at[:, b, (low, high)[way], columns(NY - k)]
            at = b * NY + 2 * way
            to_y[b, 2, way] = remote(passed, passed, w_send.at[at], w_recv.at[at], along_y(k))

    def unpack_rest(first, count):
        for at in range(first, first + count):
            for copy in to_c[at]:
                copy.wait_recv()

        def unpack(number, carry):
            cut = pl.ds(pl.multiple_of(number * width, width), width)
            pick = quarter_rows(number, False)
            for at in range(first, first + count):
                for t in range(2):
                    inbound[t, at, 4 * MAIN :, cut] = jnp.dot(
                        pick, inbound[t, at, : 4 * MAIN, features:], preferred_element_type=f32
                    ).astype(bf16)
            return carry

        lax.fori_loop(0, PARTS, unpack, 0)

    def project(first, count, turns):
        rows = count * ROWS
        stretch = pl.ds(first * ROWS, rows)
        for k in turns:
            cut = columns(NY - k)
            for m in range(3):
                left = inbound[m // 2, first : first + count, :, cut].reshape(rows, width)
                right = weights[m, :, :, cut].reshape(units, width)
                if count > 2:
                    term = lax.dot_general(
                        left, right, (((1,), (1,)), ((), ())), preferred_element_type=f32
                    )
                else:
                    term = lax.dot_general(
                        right, left, (((1,), (1,)), ((), ())), preferred_element_type=f32
                    ).T
                if k == 0:
                    pre[m, stretch] = term
                else:
                    pre[m, stretch] += term

    def activate(first, count):
        stretch = pl.ds(first * ROWS, count * ROWS)
        gate, up, hidden_cot = pre[0, stretch], pre[1, stretch], pre[2, stretch]
        sig = jax.nn.sigmoid(gate)
        activated = gate * sig
        signals[2, stretch] = (activated * up).astype(bf16)
        signals[0, stretch] = (hidden_cot * up * sig * (1.0 + gate * (1.0 - sig))).astype(bf16)
        signals[1, stretch] = (hidden_cot * activated).astype(bf16)

    def give_back(first, count, low_part, high_part):
        stretch = pl.ds(first * ROWS, count * ROWS)

        def one_part(number, carry):
            cut = pl.ds(pl.multiple_of(number * width, width), width)
            place_rows = quarter_rows(number, True)
            term = (
                jnp.dot(
                    signals[0, stretch],
                    weights[0, :, :, cut].reshape(units, width),
                    preferred_element_type=f32,
                )
                + jnp.dot(
                    signals[1, stretch],
                    weights[1, :, :, cut].reshape(units, width),
                    preferred_element_type=f32,
                )
            ).astype(bf16)
            for i in range(count):
                one = term[i * ROWS : (i + 1) * ROWS]
                terms[first + i, :, :, cut] = one[: 4 * MAIN].reshape(4, MAIN, width)
                rest[i] += jnp.dot(place_rows, one[4 * MAIN :], preferred_element_type=f32)
            return carry

        if low_part == 0:
            rest[:count] = jnp.zeros((count,) + rest.shape[1:], f32)
        lax.fori_loop(low_part, high_part, one_part, 0)
        if high_part == PARTS:
            for i in range(count):
                terms[first + i, :, :, features:] = rest[i].astype(bf16).reshape(4, MAIN, width)
            for at in range(first, first + count):
                to_e[at] = remote(
                    terms.at[at, pl.ds(2, 2)],
                    crossed.at[at],
                    e_send.at[at],
                    e_recv.at[at],
                    other_core(),
                )

    def weights_of(k):
        if k == 2:
            for b in range(2):
                for way in range(2):
                    to_y[b, 2, way].wait_recv()
        elif k == 0:
            keep_weights.wait()

    to_e, to_p, to_r = {}, {}, {}

    def fold(at):
        to_e[at].wait_recv()
        for col in (1, 0):
            terms[at, col] = (terms[at, col].astype(f32) + crossed[at, col].astype(f32)).astype(bf16)
            if col:
                to_p[at] = remote(
                    terms.at[at, 1], paired.at[at], p_send.at[at], p_recv.at[at], token_pair()
                )

    def back(at):
        to_p[at].wait_recv()
        total = (terms[at, 0].astype(f32) + paired[at].astype(f32)).astype(bf16)
        k = ORDER[at]
        if k == 0:
            returned[0] = total
        else:
            terms[at, 0] = total
            to_r[at] = remote(
                terms.at[at, 0], returned.at[k], r_send.at[at], r_recv.at[at], along_z(NZ - k)
            )

    to_g, to_f, to_h, to_s, to_b, to_t = [], [], [], [], [], []

    def half_columns(k, way):
        start = (y + k) % NY * width + way * (width // 2)
        return pl.ds(pl.multiple_of(start, width // 2), width // 2)


    def differentiate(m):
        def columns_of(number, carry):
            cut = pl.ds(pl.multiple_of(number * (width // 2), width // 2), width // 2)
            grads[m, :, :, cut] = (
                lax.dot_general(
                    signals[m],
                    inbound[m // 2, :, :, cut].reshape(NZ * ROWS, width // 2),
                    (((0,), (0,)), ((), ())),
                    preferred_element_type=f32,
                )
                .astype(bf16)
                .reshape(2, stored, width // 2)
            )
            return carry

        lax.fori_loop(0, 2 * PARTS, columns_of, 0)
        to_g.append(
            remote(grads.at[m, 1, high], from_x.at[m], g_send.at[m], g_recv.at[m], weight_pair())
        )
        for way in range(2):
            to_f.append(
                remote(
                    grads.at[m, :, low, half_columns(2, way)],
                    far_y.at[way, m],
                    f_send.at[m, way],
                    f_recv.at[m, way],
                    along_y(NEXT[way]),
                )
            )

    def near(m):
        for way in range(2):
            to_f[2 * m + way].wait_recv()
            cut = half_columns(NEXT[way], way)
            grads[m, :, low, cut] = (
                grads[m, :, low, cut].astype(f32) + far_y[way, m].astype(f32)
            ).astype(bf16)
            to_s.append(
                remote(
                    grads.at[m, :, low, columns(NEXT[way])],
                    from_y.at[way, m],
                    y_send.at[m, way],
                    y_recv.at[m, way],
                    along_y(NEXT[way]),
                )
            )

    def through(m):
        to_g[m].wait_recv()
        block[m] = (grads[m, 0, high].astype(f32) + from_x[m].astype(f32)).astype(bf16)
        for way in range(2):
            to_h.append(
                remote(
                    block.at[m, :, half_columns(2, way)],
                    far_block.at[way, m],
                    h_send.at[m, way],
                    h_recv.at[m, way],
                    along_y(NEXT[way]),
                )
            )

    def near_block(m):
        for way in range(2):
            to_h[2 * m + way].wait_recv()
            cut = half_columns(NEXT[way], way)
            block[m, :, cut] = (
                block[m, :, cut].astype(f32) + far_block[way, m].astype(f32)
            ).astype(bf16)
            to_b.append(
                remote(
                    block.at[m, :, columns(NEXT[way])],
                    from_y_block.at[way, m],
                    b_send.at[m, way],
                    b_recv.at[m, way],
                    along_y(NEXT[way]),
                )
            )

    def gather(m):
        for copy in to_s[2 * m : 2 * m + 2]:
            copy.wait_recv()
        for b in (1, 0):
            total = grads[m, b, low, mine].astype(f32)
            for way in range(2):
                total = total + from_y[way, m, b].astype(f32)
            if b:
                part[m] = total.astype(bf16)
                to_t.append(
                    remote(part.at[m], given.at[m], t_send.at[m], t_recv.at[m], weight_pair())
                )
            else:
                gradient[m, low] = total

    def finish(m):
        for copy in to_b[2 * m : 2 * m + 2]:
            copy.wait_recv()
        total = block[m, :, mine].astype(f32)
        for way in range(2):
            total = total + from_y_block[way, m].astype(f32)
        gradient[m, high] = total
        to_t[m].wait_recv()
        gradient[m, low] = gradient[m, low] + given[m].astype(f32)

    keep_rows.wait()
    spread(0)
    arrive(1)
    launch(5)
    cross(0)
    arrive(2)
    launch(6)
    weights_on()
    relay(0)
    cross(1)
    cross(2)
    arrive(3)
    launch(7)
    arrive(4)
    cross(3)
    relay(1)
    cross(4)
    unpack_rest(0, 5)
    weights_of(0)
    project(0, 5, (0,))
    weights_of(1)
    project(0, 5, (1,))
    arrive(5)
    weights_of(3)
    project(0, 5, (3,))
    arrive(6)
    cross(5)
    weights_of(2)
    project(0, 5, (2,))
    activate(0, 5)
    cross(6)
    give_back(0, 5, 0, 2)
    arrive(7)
    give_back(0, 5, 2, 4)
    unpack_rest(5, 2)
    project(5, 2, (0, 1, 3, 2))
    activate(5, 2)
    give_back(5, 2, 0, 4)
    cross(7)
    fold(6)
    fold(5)
    unpack_rest(7, 1)
    project(7, 1, (0, 1, 3, 2))
    activate(7, 1)
    differentiate(0)
    back(6)
    differentiate(1)
    back(5)
    differentiate(2)
    give_back(7, 1, 0, 4)
    fold(4)
    fold(3)
    fold(7)
    near(0)
    near(1)
    near(2)
    back(4)
    fold(2)
    fold(1)
    back(3)
    fold(0)
    through(0)
    back(7)
    near_block(0)
    back(2)
    gather(0)
    back(1)
    through(1)
    near_block(1)
    gather(1)
    back(0)
    through(2)
    gather(2)
    near_block(2)
    finish(0)
    finish(1)
    for at in range(1, NZ):
        to_r[at].wait_recv()

    def unpack_tokens(number, carry):
        cut = pl.ds(pl.multiple_of(number * width, width), width)
        token_grads[:, cut] = (
            jnp.dot(
                unpicks[PARTS],
                returned[:, :, cut].reshape(count, width),
                preferred_element_type=f32,
            )
            + jnp.dot(
                unpicks[number],
                returned[:, :, tail].reshape(count, width),
                preferred_element_type=f32,
            )
        ).astype(bf16)
        return carry

    lax.fori_loop(0, PARTS, unpack_tokens, 0)
    finish(2)
    for at in range(NZ):
        to_e[at].wait_send()
        to_p[at].wait_send()
        to_x[at].wait_send()
        for copy in to_c[at]:
            copy.wait_send()
        if at:
            to_z[at].wait_send()
            to_r[at].wait_send()
    to_partner.wait_send()
    for copy in list(to_y.values()) + to_g + to_f + to_h + to_s + to_b + to_t:
        copy.wait_send()


def expert_step(tokens, cotangent, routes, codes, scales):
    count, features = tokens.shape
    _, stored, width = codes.shape
    long = features + width
    units, half = 2 * stored, stored // 2
    dma = pltpu.SemaphoreType.DMA
    return pl.pallas_call(
        expert_kernel,
        out_shape=(
            jax.ShapeDtypeStruct((count, features), bf16),
            jax.ShapeDtypeStruct((3, stored, width), f32),
            jax.ShapeDtypeStruct((3, stored, width), f32),
        ),
        in_specs=[HBM, HBM, VMEM, VMEM, VMEM],
        out_specs=(VMEM, VMEM, VMEM),
        scratch_shapes=[
            pltpu.VMEM((NZ, 2, MAIN, long), bf16),
            pltpu.VMEM((3, stored, width), bf16),
            pltpu.VMEM((NZ, MAIN, long), bf16),
            pltpu.VMEM((PARTS, 2 * count, count), bf16),
            pltpu.VMEM((PARTS + 1, count, count), bf16),
            pltpu.VMEM((2, NZ, ROWS, long), bf16),
            pltpu.VMEM((3, 2, stored, features), bf16),
            pltpu.VMEM((3, NZ * ROWS, units), f32),
            pltpu.VMEM((3, NZ * ROWS, units), bf16),
            pltpu.VMEM((NZ, 4, MAIN, long), bf16),
            pltpu.VMEM((5, 4 * MAIN, width), f32),
            pltpu.VMEM((3, 2, stored, features), bf16),
            pltpu.VMEM((NZ, 2, MAIN, long), bf16),
            pltpu.VMEM((NZ, MAIN, long), bf16),
            pltpu.VMEM((3, half, features), bf16),
            pltpu.VMEM((3, half, features), bf16),
            pltpu.VMEM((2, 3, 2, half, width // 2), bf16),
            pltpu.VMEM((2, 3, half, width // 2), bf16),
            pltpu.VMEM((2, 3, 2, half, width), bf16),
            pltpu.VMEM((2, 3, half, width), bf16),
            pltpu.VMEM((3, half, width), bf16),
            pltpu.VMEM((3, half, width), bf16),
        ]
        + [dma((NZ,))] * 4
        + [dma((2, NZ))] * 2
        + [dma((2 * NY + 1,))] * 2
        + [dma((NZ,))] * 6
        + [dma((3,))] * 2
        + [dma((3, 2))] * 8
        + [dma((3,))] * 2
        + [dma((2,))] * 2,
        compiler_params=pltpu.CompilerParams(
            collective_id=0, has_side_effects=True, vmem_limit_bytes=62 << 20
        ),
        cost_estimate=pl.CostEstimate(flops=10 * 10**9, bytes_accessed=10**8, transcendentals=0),
        name="expert_step",
    )(
        tokens.reshape(2, 4, MAIN, features),
        cotangent.reshape(2, 4, MAIN, features),
        routes.reshape(1, count),
        codes,
        scales.transpose(0, 2, 1),
    )


def shards(tokens, cotangent, routes, codes, scales, first_moment, second_moment):
    grad_tokens, gradient, owned_full = expert_step(tokens, cotangent, routes, codes, scales)
    new_first = BETA_ONE * first_moment + (1.0 - BETA_ONE) * gradient
    new_second = BETA_TWO * second_moment + (1.0 - BETA_TWO) * gradient * gradient
    first_fix = 1.0 - BETA_ONE**STEP_COUNT
    second_fix = 1.0 - BETA_TWO**STEP_COUNT
    new_weights = owned_full - LEARNING_RATE * (new_first / first_fix) / (
        jnp.sqrt(new_second / second_fix) + ADAM_EPS
    )
    return (grad_tokens, new_weights, new_first, new_second)


def solution(mesh):
    stored = P(None, "dev", "group")
    spread = P(("group", "dev"), None)
    return jax.shard_map(
        shards,
        mesh=mesh,
        in_specs=(spread, spread, spread, stored, stored, stored, stored),
        out_specs=(spread, stored, stored, stored),
        check_vma=False,
    )
```

```python
import jax
import jax.numpy as jnp
from jax import lax
from jax.experimental import pallas as pl
from jax.experimental.pallas import tpu as pltpu
from jax.sharding import PartitionSpec as P

MESH = pl.DeviceIdType.MESH
QB = 128
NZ, NX, NY = 8, 4, 4
CAP = 20
MAIN, REST = 16, 4
PARTS = 4
ROWS = 4 * CAP
NEXT = (1, 3)
ORDER = (0, 1, 7, 2, 6, 3, 5, 4)
HBM = pl.BlockSpec(memory_space=pltpu.HBM)
VMEM = pl.BlockSpec(memory_space=pltpu.VMEM)

BETA_ONE = 0.9
BETA_TWO = 0.999
LEARNING_RATE = 0.01
ADAM_EPS = 1e-08
STEP_COUNT = 10

f32, bf16 = jnp.float32, jnp.bfloat16


def place():
    dev = lax.axis_index("dev")
    return lax.axis_index("group"), dev // 8, (dev // 2) % 4, dev % 2


def device(y, z, x, c):
    return (y, (z * NX + x) * 2 + c)


def along_z(k):
    y, z, x, c = place()
    return device(y, (z + k) % NZ, x, c)


def along_y(k):
    y, z, x, c = place()
    return device((y + k) % NY, z, x, c)


def token_pair():
    y, z, x, c = place()
    return device(y, z, x + 1 - 2 * (x % 2), c)


def weight_pair():
    y, z, x, c = place()
    return device(y, z, 3 - x, c)


def other_core():
    y, z, x, c = place()
    return device(y, z, x, 1 - c)


def remote(src, dst, send, recv, peer):
    copy = pltpu.make_async_remote_copy(src, dst, send, recv, device_id=peer, device_id_type=MESH)
    copy.start()
    return copy


def quarter_rows(part, rows_first):
    shape = (4 * MAIN, MAIN) if rows_first else (MAIN, 4 * MAIN)
    row = lax.broadcasted_iota(jnp.int32, shape, 0 if rows_first else 1)
    slot = lax.broadcasted_iota(jnp.int32, shape, 1 if rows_first else 0)
    source, inner = slot // REST, slot % REST
    return jnp.where(row == source * MAIN + part * REST + inner, 1.0, 0.0).astype(bf16)


def expert_kernel(
    tokens, cotangent, routes, codes, scales, token_grads, gradient, full,
    slabs, owned, returned, picks, unpicks, inbound, weights, pre, signals, terms, rest, grads, crossed, paired,
    from_x, block, far_y, far_block, from_y, from_y_block, part, given,
    z_send, z_recv, x_send, x_recv, c_send, c_recv, w_send, w_recv,
    e_send, e_recv, p_send, p_recv, r_send, r_recv,
    g_send, g_recv, f_send, f_recv, h_send, h_recv, y_send, y_recv, b_send, b_recv, t_send, t_recv, local, load,
):
    y = lax.axis_index("group")
    stored, width = owned.shape[1:]
    features = weights.shape[3]
    tail = pl.ds(features, width)
    units = 2 * stored
    half = stored // 2
    low, high = pl.ds(0, half), pl.ds(half, half)

    def columns(k):
        return pl.ds(pl.multiple_of((y + k) % NY * width, width), width)

    mine = columns(0)

    def source_rows(number):
        return pl.ds(number * MAIN, MAIN)

    peers = (
        [along_z(k) for k in range(1, NZ)]
        + [along_y(k) for k in range(1, NY)]
        + [token_pair(), weight_pair(), other_core()]
    )
    barrier = pltpu.get_barrier_semaphore()
    for peer in peers:
        pl.semaphore_signal(barrier, inc=1, device_id=peer, device_id_type=MESH)

    loads = []
    for t, source in enumerate((tokens, cotangent)):
        loads.append(
            pltpu.make_async_copy(
                source, terms.at[pl.ds(2 * t, 2), :, :, pl.ds(0, features)], load.at[t]
            )
        )
        loads[t].start()
    for m in range(3):
        columned = scales[m].T
        for b in range(scales.shape[1]):
            cut = pl.ds(b * QB, QB)
            full[m, :, cut] = codes[m, :, cut].astype(f32) * columned[:, b : b + 1]
            owned[m, :, cut] = full[m, :, cut].astype(bf16)

    count = routes.shape[1]
    _, z, _, _ = place()
    row_range = lax.broadcasted_iota(jnp.int32, (count, count), 0)
    column_range = lax.broadcasted_iota(jnp.int32, (count, count), 1)
    before = jnp.where(row_range < column_range, 1.0, 0.0).astype(bf16)
    matches = lax.broadcasted_iota(jnp.int32, (MAIN, count), 0) == routes[...]
    earlier = jnp.dot(
        jnp.where(matches, 1.0, 0.0).astype(bf16), before, preferred_element_type=f32
    )
    position = jnp.sum(jnp.where(matches, earlier, 0.0), axis=0, keepdims=True).astype(jnp.int32)
    first_slot = (routes[...] - z + NZ) % NZ * MAIN
    in_main = position < MAIN
    main = jnp.where(row_range == jnp.where(in_main, first_slot + position, -1), 1.0, 0.0)
    unpicks[PARTS] = main.T.astype(bf16)
    for number in range(PARTS):
        slot = jnp.where(in_main, -1, first_slot + number * REST + position - MAIN)
        pick = jnp.where(row_range == slot, 1.0, 0.0)
        picks[number, :count] = main.astype(bf16)
        picks[number, count:] = pick.astype(bf16)
        unpicks[number] = pick.T.astype(bf16)

    pl.semaphore_wait(barrier, len(peers))

    to_partner = remote(
        owned, weights.at[:, 1, :, mine], w_send.at[2 * NY], w_recv.at[2 * NY], weight_pair()
    )
    keep_weights = pltpu.make_async_copy(owned, weights.at[:, 0, :, mine], local.at[1])
    keep_weights.start()
    to_y = {
        (0, k): remote(owned, weights.at[:, 0, :, mine], w_send.at[k], w_recv.at[k], along_y(k))
        for k in NEXT
    }
    for t in range(2):
        loads[t].wait()

        def pack(number, carry):
            cut = pl.ds(pl.multiple_of(number * width, width), width)
            values = terms[2 * t : 2 * t + 2, :, :, cut].reshape(count, width)
            packed = jnp.dot(
                picks[number], values, preferred_element_type=f32
            ).astype(bf16)
            slabs[:, t, :, cut] = packed[:count].reshape(NZ, MAIN, width)
            slabs[:, t, :, tail] = slabs[:, t, :, tail] + packed[count:].reshape(NZ, MAIN, width)
            return carry

        slabs[:, t, :, tail] = jnp.zeros((NZ, MAIN, width), bf16)
        lax.fori_loop(0, PARTS, pack, 0)
    keep_rows = pltpu.make_async_copy(
        slabs.at[0], inbound.at[:, 0, source_rows(0)], local.at[0]
    )
    keep_rows.start()
    to_z = [None]
    def launch(at):
        k = ORDER[at]
        to_z.append(
            remote(
                slabs.at[k],
                inbound.at[:, at, source_rows(0)],
                z_send.at[at],
                z_recv.at[at],
                along_z(k),
            )
        )
    for at in range(1, 5):
        launch(at)
    to_x, to_c = [], []

    def spread(at):
        own = inbound.at[:, at, source_rows(0)]
        to_x.append(
            remote(
                own,
                inbound.at[:, at, source_rows(1)],
                x_send.at[at],
                x_recv.at[at],
                token_pair(),
            )
        )
        to_c.append(
            [
                remote(
                    own,
                    inbound.at[:, at, source_rows(2)],
                    c_send.at[0, at],
                    c_recv.at[0, at],
                    other_core(),
                )
            ]
        )

    def cross(at):
        to_x[at].wait_recv()
        to_c[at].append(
            remote(
                inbound.at[:, at, source_rows(1)],
                inbound.at[:, at, source_rows(3)],
                c_send.at[1, at],
                c_recv.at[1, at],
                other_core(),
            )
        )

    def arrive(at):
        to_z[at].wait_recv()
        spread(at)

    def weights_on():
        to_partner.wait_recv()
        for k in NEXT:
            to_y[1, k] = remote(
                weights.at[:, 1, :, mine],
                weights.at[:, 1, :, mine],
                w_send.at[NY + k],
                w_recv.at[NY + k],
                along_y(k),
            )

    def relay(b):
        for way, k in enumerate(NEXT):
            to_y[b, k].wait_recv()
            passed = weights.at[:, b, (low, high)[way], columns(NY - k)]
            at = b * NY + 2 * way
            to_y[b, 2, way] = remote(passed, passed, w_send.at[at], w_recv.at[at], along_y(k))

    def unpack_rest(first, count):
        for at in range(first, first + count):
            for copy in to_c[at]:
                copy.wait_recv()

        def unpack(number, carry):
            cut = pl.ds(pl.multiple_of(number * width, width), width)
            pick = quarter_rows(number, False)
            for at in range(first, first + count):
                for t in range(2):
                    inbound[t, at, 4 * MAIN :, cut] = jnp.dot(
                        pick, inbound[t, at, : 4 * MAIN, features:], preferred_element_type=f32
                    ).astype(bf16)
            return carry

        lax.fori_loop(0, PARTS, unpack, 0)

    def project(first, count, turns):
        rows = count * ROWS
        stretch = pl.ds(first * ROWS, rows)
        for k in turns:
            cut = columns(NY - k)
            for m in range(3):
                left = inbound[m // 2, first : first + count, :, cut].reshape(rows, width)
                right = weights[m, :, :, cut].reshape(units, width)
                if count > 2:
                    term = lax.dot_general(
                        left, right, (((1,), (1,)), ((), ())), preferred_element_type=f32
                    )
                else:
                    term = lax.dot_general(
                        right, left, (((1,), (1,)), ((), ())), preferred_element_type=f32
                    ).T
                if k == 0:
                    pre[m, stretch] = term
                else:
                    pre[m, stretch] += term

    def activate(first, count):
        stretch = pl.ds(first * ROWS, count * ROWS)
        gate, up, hidden_cot = pre[0, stretch], pre[1, stretch], pre[2, stretch]
        sig = jax.nn.sigmoid(gate)
        activated = gate * sig
        signals[2, stretch] = (activated * up).astype(bf16)
        signals[0, stretch] = (hidden_cot * up * sig * (1.0 + gate * (1.0 - sig))).astype(bf16)
        signals[1, stretch] = (hidden_cot * activated).astype(bf16)

    def give_back(first, count, low_part, high_part):
        stretch = pl.ds(first * ROWS, count * ROWS)

        def one_part(number, carry):
            cut = pl.ds(pl.multiple_of(number * width, width), width)
            place_rows = quarter_rows(number, True)
            term = (
                jnp.dot(
                    signals[0, stretch],
                    weights[0, :, :, cut].reshape(units, width),
                    preferred_element_type=f32,
                )
                + jnp.dot(
                    signals[1, stretch],
                    weights[1, :, :, cut].reshape(units, width),
                    preferred_element_type=f32,
                )
            ).astype(bf16)
            for i in range(count):
                one = term[i * ROWS : (i + 1) * ROWS]
                terms[first + i, :, :, cut] = one[: 4 * MAIN].reshape(4, MAIN, width)
                rest[i] += jnp.dot(place_rows, one[4 * MAIN :], preferred_element_type=f32)
            return carry

        if low_part == 0:
            rest[:count] = jnp.zeros((count,) + rest.shape[1:], f32)
        lax.fori_loop(low_part, high_part, one_part, 0)
        if high_part == PARTS:
            for i in range(count):
                terms[first + i, :, :, features:] = rest[i].astype(bf16).reshape(4, MAIN, width)
            for at in range(first, first + count):
                to_e[at] = remote(
                    terms.at[at, pl.ds(2, 2)],
                    crossed.at[at],
                    e_send.at[at],
                    e_recv.at[at],
                    other_core(),
                )

    def weights_of(k):
        if k == 2:
            for b in range(2):
                for way in range(2):
                    to_y[b, 2, way].wait_recv()
        elif k == 0:
            keep_weights.wait()

    to_e, to_p, to_r = {}, {}, {}

    def fold(at):
        to_e[at].wait_recv()
        for col in (1, 0):
            terms[at, col] = (terms[at, col].astype(f32) + crossed[at, col].astype(f32)).astype(bf16)
            if col:
                to_p[at] = remote(
                    terms.at[at, 1], paired.at[at], p_send.at[at], p_recv.at[at], token_pair()
                )

    def back(at):
        to_p[at].wait_recv()
        total = (terms[at, 0].astype(f32) + paired[at].astype(f32)).astype(bf16)
        k = ORDER[at]
        if k == 0:
            returned[0] = total
        else:
            terms[at, 0] = total
            to_r[at] = remote(
                terms.at[at, 0], returned.at[k], r_send.at[at], r_recv.at[at], along_z(NZ - k)
            )

    to_g, to_f, to_h, to_s, to_b, to_t = [], [], [], [], [], []

    def half_columns(k, way):
        start = (y + k) % NY * width + way * (width // 2)
        return pl.ds(pl.multiple_of(start, width // 2), width // 2)


    def differentiate(m):
        def columns_of(number, carry):
            cut = pl.ds(pl.multiple_of(number * (width // 2), width // 2), width // 2)
            grads[m, :, :, cut] = (
                lax.dot_general(
                    signals[m],
                    inbound[m // 2, :, :, cut].reshape(NZ * ROWS, width // 2),
                    (((0,), (0,)), ((), ())),
                    preferred_element_type=f32,
                )
                .astype(bf16)
                .reshape(2, stored, width // 2)
            )
            return carry

        lax.fori_loop(0, 2 * PARTS, columns_of, 0)
        to_g.append(
            remote(grads.at[m, 1, high], from_x.at[m], g_send.at[m], g_recv.at[m], weight_pair())
        )
        for way in range(2):
            to_f.append(
                remote(
                    grads.at[m, :, low, half_columns(2, way)],
                    far_y.at[way, m],
                    f_send.at[m, way],
                    f_recv.at[m, way],
                    along_y(NEXT[way]),
                )
            )

    def near(m):
        for way in range(2):
            to_f[2 * m + way].wait_recv()
            cut = half_columns(NEXT[way], way)
            grads[m, :, low, cut] = (
                grads[m, :, low, cut].astype(f32) + far_y[way, m].astype(f32)
            ).astype(bf16)
            to_s.append(
                remote(
                    grads.at[m, :, low, columns(NEXT[way])],
                    from_y.at[way, m],
                    y_send.at[m, way],
                    y_recv.at[m, way],
                    along_y(NEXT[way]),
                )
            )

    def through(m):
        to_g[m].wait_recv()
        block[m] = (grads[m, 0, high].astype(f32) + from_x[m].astype(f32)).astype(bf16)
        for way in range(2):
            to_h.append(
                remote(
                    block.at[m, :, half_columns(2, way)],
                    far_block.at[way, m],
                    h_send.at[m, way],
                    h_recv.at[m, way],
                    along_y(NEXT[way]),
                )
            )

    def near_block(m):
        for way in range(2):
            to_h[2 * m + way].wait_recv()
            cut = half_columns(NEXT[way], way)
            block[m, :, cut] = (
                block[m, :, cut].astype(f32) + far_block[way, m].astype(f32)
            ).astype(bf16)
            to_b.append(
                remote(
                    block.at[m, :, columns(NEXT[way])],
                    from_y_block.at[way, m],
                    b_send.at[m, way],
                    b_recv.at[m, way],
                    along_y(NEXT[way]),
                )
            )

    def gather(m):
        for copy in to_s[2 * m : 2 * m + 2]:
            copy.wait_recv()
        for b in (1, 0):
            total = grads[m, b, low, mine].astype(f32)
            for way in range(2):
                total = total + from_y[way, m, b].astype(f32)
            if b:
                part[m] = total.astype(bf16)
                to_t.append(
                    remote(part.at[m], given.at[m], t_send.at[m], t_recv.at[m], weight_pair())
                )
            else:
                gradient[m, low] = total

    def finish(m):
        for copy in to_b[2 * m : 2 * m + 2]:
            copy.wait_recv()
        total = block[m, :, mine].astype(f32)
        for way in range(2):
            total = total + from_y_block[way, m].astype(f32)
        gradient[m, high] = total
        to_t[m].wait_recv()
        gradient[m, low] = gradient[m, low] + given[m].astype(f32)

    keep_rows.wait()
    spread(0)
    arrive(1)
    launch(5)
    cross(0)
    arrive(2)
    launch(6)
    weights_on()
    relay(0)
    cross(1)
    cross(2)
    arrive(3)
    launch(7)
    arrive(4)
    cross(3)
    relay(1)
    cross(4)
    unpack_rest(0, 5)
    weights_of(0)
    project(0, 5, (0,))
    weights_of(1)
    project(0, 5, (1,))
    arrive(5)
    weights_of(3)
    project(0, 5, (3,))
    arrive(6)
    cross(5)
    weights_of(2)
    project(0, 5, (2,))
    activate(0, 5)
    cross(6)
    give_back(0, 5, 0, 2)
    arrive(7)
    give_back(0, 5, 2, 4)
    unpack_rest(5, 2)
    project(5, 2, (0, 1, 3, 2))
    activate(5, 2)
    give_back(5, 2, 0, 4)
    cross(7)
    fold(6)
    fold(5)
    unpack_rest(7, 1)
    project(7, 1, (0, 1, 3, 2))
    activate(7, 1)
    differentiate(0)
    back(6)
    differentiate(1)
    back(5)
    differentiate(2)
    give_back(7, 1, 0, 4)
    fold(4)
    fold(3)
    near(0)
    near(1)
    fold(7)
    near(2)
    back(4)
    fold(2)
    fold(1)
    back(3)
    fold(0)
    through(0)
    back(7)
    near_block(0)
    back(2)
    gather(0)
    back(1)
    through(1)
    near_block(1)
    gather(1)
    back(0)
    through(2)
    gather(2)
    near_block(2)
    finish(0)
    finish(1)
    for at in range(1, NZ):
        to_r[at].wait_recv()

    def unpack_tokens(number, carry):
        cut = pl.ds(pl.multiple_of(number * width, width), width)
        token_grads[:, cut] = (
            jnp.dot(
                unpicks[PARTS],
                returned[:, :, cut].reshape(count, width),
                preferred_element_type=f32,
            )
            + jnp.dot(
                unpicks[number],
                returned[:, :, tail].reshape(count, width),
                preferred_element_type=f32,
            )
        ).astype(bf16)
        return carry

    lax.fori_loop(0, PARTS, unpack_tokens, 0)
    finish(2)
    for at in range(NZ):
        to_e[at].wait_send()
        to_p[at].wait_send()
        to_x[at].wait_send()
        for copy in to_c[at]:
            copy.wait_send()
        if at:
            to_z[at].wait_send()
            to_r[at].wait_send()
    to_partner.wait_send()
    for copy in list(to_y.values()) + to_g + to_f + to_h + to_s + to_b + to_t:
        copy.wait_send()


def expert_step(tokens, cotangent, routes, codes, scales):
    count, features = tokens.shape
    _, stored, width = codes.shape
    long = features + width
    units, half = 2 * stored, stored // 2
    dma = pltpu.SemaphoreType.DMA
    return pl.pallas_call(
        expert_kernel,
        out_shape=(
            jax.ShapeDtypeStruct((count, features), bf16),
            jax.ShapeDtypeStruct((3, stored, width), f32),
            jax.ShapeDtypeStruct((3, stored, width), f32),
        ),
        in_specs=[HBM, HBM, VMEM, VMEM, VMEM],
        out_specs=(VMEM, VMEM, VMEM),
        scratch_shapes=[
            pltpu.VMEM((NZ, 2, MAIN, long), bf16),
            pltpu.VMEM((3, stored, width), bf16),
            pltpu.VMEM((NZ, MAIN, long), bf16),
            pltpu.VMEM((PARTS, 2 * count, count), bf16),
            pltpu.VMEM((PARTS + 1, count, count), bf16),
            pltpu.VMEM((2, NZ, ROWS, long), bf16),
            pltpu.VMEM((3, 2, stored, features), bf16),
            pltpu.VMEM((3, NZ * ROWS, units), f32),
            pltpu.VMEM((3, NZ * ROWS, units), bf16),
            pltpu.VMEM((NZ, 4, MAIN, long), bf16),
            pltpu.VMEM((5, 4 * MAIN, width), f32),
            pltpu.VMEM((3, 2, stored, features), bf16),
            pltpu.VMEM((NZ, 2, MAIN, long), bf16),
            pltpu.VMEM((NZ, MAIN, long), bf16),
            pltpu.VMEM((3, half, features), bf16),
            pltpu.VMEM((3, half, features), bf16),
            pltpu.VMEM((2, 3, 2, half, width // 2), bf16),
            pltpu.VMEM((2, 3, half, width // 2), bf16),
            pltpu.VMEM((2, 3, 2, half, width), bf16),
            pltpu.VMEM((2, 3, half, width), bf16),
            pltpu.VMEM((3, half, width), bf16),
            pltpu.VMEM((3, half, width), bf16),
        ]
        + [dma((NZ,))] * 4
        + [dma((2, NZ))] * 2
        + [dma((2 * NY + 1,))] * 2
        + [dma((NZ,))] * 6
        + [dma((3,))] * 2
        + [dma((3, 2))] * 8
        + [dma((3,))] * 2
        + [dma((2,))] * 2,
        compiler_params=pltpu.CompilerParams(
            collective_id=0, has_side_effects=True, vmem_limit_bytes=62 << 20
        ),
        cost_estimate=pl.CostEstimate(flops=10 * 10**9, bytes_accessed=10**8, transcendentals=0),
        name="expert_step",
    )(
        tokens.reshape(2, 4, MAIN, features),
        cotangent.reshape(2, 4, MAIN, features),
        routes.reshape(1, count),
        codes,
        scales.transpose(0, 2, 1),
    )


def shards(tokens, cotangent, routes, codes, scales, first_moment, second_moment):
    grad_tokens, gradient, owned_full = expert_step(tokens, cotangent, routes, codes, scales)
    new_first = BETA_ONE * first_moment + (1.0 - BETA_ONE) * gradient
    new_second = BETA_TWO * second_moment + (1.0 - BETA_TWO) * gradient * gradient
    first_fix = 1.0 - BETA_ONE**STEP_COUNT
    second_fix = 1.0 - BETA_TWO**STEP_COUNT
    new_weights = owned_full - LEARNING_RATE * (new_first / first_fix) / (
        jnp.sqrt(new_second / second_fix) + ADAM_EPS
    )
    return (grad_tokens, new_weights, new_first, new_second)


def solution(mesh):
    stored = P(None, "dev", "group")
    spread = P(("group", "dev"), None)
    return jax.shard_map(
        shards,
        mesh=mesh,
        in_specs=(spread, spread, spread, stored, stored, stored, stored),
        out_specs=(spread, stored, stored, stored),
        check_vma=False,
    )
```
